32 devices in a mesh: row: 16 (over z, y, core), hid: 2 (over x).
Axes of the slice: x: 2, y: 2, z: 4, core: 2. Of those that a mesh axis runs over, the one named last changes fastest.
Arguments:
- features: bfloat16 [64, 256, 512], P('row'), may hold values from -6 to 6
- dw_weight: float32 [2, 7, 7, 512], replicated, may hold values from -0.875 to 0.875
- dw_bias: float32 [2, 512], replicated, may hold values from -3 to 3
- ln_gain: float32 [2, 512], replicated, may hold values from 0.1 to 1.9
- ln_bias: float32 [2, 512], replicated, may hold values from -3 to 3
- w_up: bfloat16 [2, 512, 2048], P(None, None, 'hid'), may hold values from -0.25 to 0.25
- b_up: float32 [2, 2048], P(None, 'hid'), may hold values from -3 to 3
- w_down: bfloat16 [2, 2048, 512], P(None, 'hid'), may hold values from -0.125 to 0.125
- b_down: float32 [2, 512], replicated, may hold values from -3 to 3
- layer_scale: float32 [2, 512], replicated, may hold values from 0.2 to 1
Outputs:
- result_map: bfloat16 [64, 256, 512], P('row')
The draws below stay inside these ranges and needn't reach their ends.
All inputs are finite; a program needn't handle non-finite values.
Results may differ from the reference program's by a relative error of at most 0.018.
Values may be sent and summed in bfloat16 or wider, within the bound.
No kernel may reach another device: no remote copies, remote signals or barrier semaphores. Data moves between devices by JAX's collectives and lax.ppermute only.
A program may use at most 64 MiB of HBM per device.

```python
import math
import jax
import jax.numpy as jnp
from jax import lax

C = 512
FF = 2048
WIDTH = 256
BLOCKS = 2
KSIZE = 7
HEIGHT = 64
FF_DEV = 1024


def block_scale(stream_key, dims, shards, smallest, largest):
    loudness, own = 1.0, jax.random.fold_in(stream_key, 6)
    for position, parts in shards:
        heights = jnp.exp(jax.random.uniform(jax.random.fold_in(own, position), (parts,), jnp.float32, smallest / len(shards), largest / len(shards)))
        loudness = loudness * jnp.repeat(heights, dims[position] // parts).reshape([-1 if axis == position else 1 for axis in range(len(dims))])
    return loudness


def bell_draw(key, shape, scale, limit, shards=(), kind=jnp.bfloat16):
    drawn = jax.random.normal(key, shape, jnp.float32) * scale
    if len(shards) > 0:
        drawn = block_scale(key, shape, shards, -0.22, 0.18) * drawn
    return jnp.clip(drawn, min=-limit, max=limit).astype(kind)


def setup_inputs(seed: int = 0) -> dict:
    arg_keys = jax.random.split(jax.random.key(seed), 11)
    features = bell_draw(arg_keys[0], (HEIGHT, WIDTH, C), 1.0, 6.0, ((0, 16),))
    dw_weight = bell_draw(arg_keys[1], (BLOCKS, KSIZE, KSIZE, C), (KSIZE * KSIZE) ** -0.5, 0.875, (), jnp.float32)
    dw_bias = bell_draw(arg_keys[2], (BLOCKS, C), 0.5, 3.0, (), jnp.float32)
    ln_gain = jnp.clip(1.0 + 0.18 * jax.random.normal(arg_keys[3], (BLOCKS, C), jnp.float32), 0.1, 1.9)
    ln_bias = bell_draw(arg_keys[4], (BLOCKS, C), 0.5, 3.0, (), jnp.float32)
    w_up = bell_draw(arg_keys[5], (BLOCKS, C, FF), C ** -0.5, 0.25, ((2, 2),))
    b_up = bell_draw(arg_keys[6], (BLOCKS, FF), 0.5, 3.0, ((1, 2),), jnp.float32)
    w_down = bell_draw(arg_keys[7], (BLOCKS, FF, C), FF ** -0.5, 0.125, ((1, 2),))
    b_down = bell_draw(arg_keys[8], (BLOCKS, C), 0.5, 3.0, (), jnp.float32)
    layer_scale = jnp.clip(jnp.exp(jax.random.uniform(arg_keys[9], (BLOCKS, C), jnp.float32, math.log(0.2), math.log(1.0))), 0.2, 1.0)
    return {"features": features, "dw_weight": dw_weight, "dw_bias": dw_bias, "ln_gain": ln_gain, "ln_bias": ln_bias, "w_up": w_up, "b_up": b_up, "w_down": w_down, "b_down": b_down, "layer_scale": layer_scale}


def depthwise(state, kernel, bias):
    pad = KSIZE // 2
    padded = jnp.pad(state.astype(jnp.float32), ((pad, pad), (pad, pad), (0, 0)))
    height, width = (state.shape[0], state.shape[1])
    total = jnp.zeros(state.shape, jnp.float32)
    for i in range(KSIZE):
        for j in range(KSIZE):
            total = total + padded[i:i + height, j:j + width, :] * kernel[i, j]
    return (total + bias).astype(jnp.bfloat16)

def reference(features, dw_weight, dw_bias, ln_gain, ln_bias, w_up, b_up, w_down, b_down, layer_scale):
    state = features
    for b in range(BLOCKS):
        conv = depthwise(state, dw_weight[b], dw_bias[b]).reshape(-1, C)
        values = conv.astype(jnp.float32)
        mean = lax.optimization_barrier(jnp.mean(values, axis=1, keepdims=True))
        var = lax.optimization_barrier(jnp.mean((values - mean) ** 2, axis=1, keepdims=True))
        normed = ((values - mean) / jnp.sqrt(var + 1e-06) * ln_gain[b] + ln_bias[b]).astype(jnp.bfloat16)
        hidden = jax.nn.gelu(jnp.dot(normed, w_up[b], preferred_element_type=jnp.float32) + b_up[b], approximate=False).astype(jnp.bfloat16)
        projected = jnp.zeros((hidden.shape[0], C), jnp.float32)
        for g in range(FF // FF_DEV):
            part = jnp.dot(hidden[:, g * FF_DEV:(g + 1) * FF_DEV], w_down[b, g * FF_DEV:(g + 1) * FF_DEV, :], preferred_element_type=jnp.float32)
            projected = projected + part.astype(jnp.bfloat16).astype(jnp.float32)
        flat = state.reshape(-1, C).astype(jnp.float32)
        state = (flat + layer_scale[b] * (projected + b_down[b])).astype(jnp.bfloat16).reshape(state.shape)
    return state
```

```python
import functools

import jax
import jax.numpy as jnp
from jax import lax
from jax.experimental import pallas as pl
from jax.experimental.pallas import tpu as pltpu
from jax.sharding import PartitionSpec as P

LANES = 128
MARGIN = 16
ERF = (
    0.7978842161099958,
    0.03633428353366734,
    -3.3130008237205104e-05,
    -5.524015421773868e-05,
    3.969108888631555e-06,
    -1.33446374821295e-07,
    1.8056156531812635e-09,
)
VMEM = pl.BlockSpec(memory_space=pltpu.VMEM)
SMEM = pl.BlockSpec(memory_space=pltpu.SMEM)
PARAMS = pltpu.CompilerParams(vmem_limit_bytes=48 * 1024 * 1024)


def gelu(u):
    v = u * u
    p = jnp.full_like(u, ERF[-1])
    for c in ERF[-2::-1]:
        p = p * v + c
    half = 0.5 * u
    return half * jnp.tanh(u * p) + half


def tile_of(width):
    return next(s for s in (48, 32, 16) if width % s == 0)


def own_kernel(b, place, own, taps, bias, out, wide):
    groups, rows, width, _ = out.shape
    size = taps.shape[1]
    reach = size // 2
    for k in range(width // MARGIN + 2):
        at = place[0] + (k - 1) * MARGIN
        inside = (at >= 0) & (at <= own.shape[1] - MARGIN)
        at = pl.multiple_of(jnp.clip(at, 0, own.shape[1] - MARGIN), MARGIN)
        for r in range(rows):
            for c in range(groups):
                x = own[r, pl.ds(at, MARGIN), c * LANES : (c + 1) * LANES].astype(jnp.float32)
                wide[c, r, k * MARGIN : (k + 1) * MARGIN] = jnp.where(inside, x, 0.0)
    step = tile_of(width)

    def group(c, _):
        lanes = pl.ds(pl.multiple_of(c * LANES, LANES), LANES)
        for start in range(0, width, step):
            sums = [jnp.broadcast_to(bias[b : b + 1, lanes], (step, LANES)) for _ in range(rows)]
            for i in range(rows):
                for j in range(size):
                    first = start + MARGIN + j - reach
                    x = wide[c, i, first : first + step]
                    for r in range(rows):
                        t = i - r + reach
                        if 0 <= t < size:
                            sums[r] = sums[r] + x * taps[b, t, j : j + 1, lanes]
            for r in range(rows):
                out[c, r, start : start + step] = sums[r]
        return 0

    lax.fori_loop(0, groups, group, 0)


def add_halo(b, place, near, far, before, taps, conv, wide):
    groups, rows, width, _ = conv.shape
    size = taps.shape[1]
    reach = size // 2
    wide[...] = jnp.zeros(wide.shape, jnp.float32)
    at = pl.ds(pl.multiple_of(place[1], MARGIN), near.shape[1])
    odd = place[2]
    for c in range(groups):
        for k in range(reach):
            lanes = slice(c * LANES, (c + 1) * LANES)
            wide[c, (1 - odd) * reach + k, at] = near[k, :, lanes].astype(jnp.float32)
            wide[c, odd * reach + k, at] = far[k, :, lanes].astype(jnp.float32)
    step = tile_of(width)

    def group(c, _):
        lanes = pl.ds(pl.multiple_of(c * LANES, LANES), LANES)
        for start in range(0, width, step):
            sums = [before[c, r, start : start + step] for r in range(rows)]
            for i in range(2 * reach):
                row = i - reach if i < reach else i - reach + rows
                for j in range(size):
                    first = start + MARGIN + j - reach
                    x = wide[c, i, first : first + step]
                    for r in range(rows):
                        t = row - r + reach
                        if 0 <= t < size:
                            sums[r] = sums[r] + x * taps[b, t, j : j + 1, lanes]
            for r in range(rows):
                conv[c, r, start : start + step] = sums[r]
        return 0

    lax.fori_loop(0, groups, group, 0)


def normalise(b, conv, gain, shift, out):
    groups, rows, width, _ = conv.shape
    channels = groups * LANES
    for r in range(rows):
        x = [conv[c, r].astype(jnp.bfloat16).astype(jnp.float32) for c in range(groups)]
        mean = jnp.sum(functools.reduce(jnp.add, x), axis=1, keepdims=True) * (1.0 / channels)
        x = [v - mean for v in x]
        var = jnp.sum(functools.reduce(jnp.add, [v * v for v in x]), axis=1, keepdims=True)
        scale = lax.rsqrt(var * (1.0 / channels) + 1e-06)
        for c in range(groups):
            lanes = slice(c * LANES, (c + 1) * LANES)
            y = x[c] * scale * gain[b : b + 1, lanes] + shift[b : b + 1, lanes]
            out[r * width : (r + 1) * width, lanes] = y.astype(out.dtype)


def project(x, up, b_up, down, total, before=None):
    hidden = down.shape[0]
    part = 256 if hidden % 256 == 0 else 128
    for k in range(0, hidden, part):
        u = jnp.dot(x[...], up[:, k : k + part], preferred_element_type=jnp.float32)
        h = gelu(u + b_up[:, k : k + part]).astype(jnp.bfloat16)
        y = jnp.dot(h, down[k : k + part, :], preferred_element_type=jnp.float32)
        if k:
            total[...] += y
        else:
            total[...] = y if before is None else before[...] + y


def rest_kernel(
    b, place, near, far, before, taps, gain, shift, up, b_up, down, normed, total, conv, wide
):
    add_halo(b, place, near, far, before, taps, conv, wide)
    normalise(b, conv, gain, shift, normed)
    project(normed, up.at[b], b_up.at[b : b + 1], down.at[b], total)


def more_kernel(b, kind, last, place, x, before, *refs):
    channels = x.shape[1]
    if kind == "plain":
        up, b_up, down, *refs = refs
        b_up = b_up[...]
    else:
        if kind == "halves":
            mine, other, down, *refs = refs
            up = refs.pop()
            half = channels // 2
            up[pl.ds(pl.multiple_of(place[3] * half, half), half), :] = mine[...]
            up[pl.ds(pl.multiple_of((1 - place[3]) * half, half), half), :] = other[...]
        else:
            packed, *refs = refs
            up, down = packed.at[:channels], packed.at[channels:]
        hidden = down.shape[0] - MARGIN
        terms = down[hidden:, :].astype(jnp.float32)
        b_up, down = terms[0:1] + terms[1:2], down.at[:hidden]
    if not last:
        project(x, up, b_up, down, refs[0], before)
        return
    state, b_down, scale, out, total = refs
    project(x, up, b_up, down, total, before)
    rows, width, _ = out.shape
    for r in range(rows):
        s = state[r, pl.ds(pl.multiple_of(place[0], MARGIN), width), :].astype(jnp.float32)
        y = total[r * width : (r + 1) * width, :] + b_down[b : b + 1]
        out[r] = (s + scale[b : b + 1] * y).astype(out.dtype)


def cost(flops, transcendentals=0):
    return pl.CostEstimate(flops=flops, bytes_accessed=flops // 512, transcendentals=transcendentals)


def conv_own(b, place, own, width, taps, bias):
    rows, _, channels = own.shape
    groups = channels // LANES
    return pl.pallas_call(
        functools.partial(own_kernel, b),
        out_shape=jax.ShapeDtypeStruct((groups, rows, width, LANES), jnp.float32),
        in_specs=[SMEM] + [VMEM] * 3,
        out_specs=VMEM,
        scratch_shapes=[pltpu.VMEM((groups, rows, width + 2 * MARGIN, LANES), jnp.float32)],
        compiler_params=PARAMS,
        cost_estimate=cost(56 * rows * rows * width * channels),
        name="conv_own",
    )(place, own, taps, bias)


def conv_rest(b, place, near, far, before, taps, gain, shift, up, b_up, down):
    groups, rows, width, _ = before.shape
    channels, reach = groups * LANES, near.shape[0]
    positions = rows * width
    return pl.pallas_call(
        functools.partial(rest_kernel, b),
        out_shape=(
            jax.ShapeDtypeStruct((positions, channels), jnp.bfloat16),
            jax.ShapeDtypeStruct((positions, channels), jnp.float32),
        ),
        in_specs=[SMEM] + [VMEM] * 9,
        out_specs=(VMEM, VMEM),
        scratch_shapes=[
            pltpu.VMEM((groups, rows, width, LANES), jnp.float32),
            pltpu.VMEM((groups, 2 * reach, width + 2 * MARGIN, LANES), jnp.float32),
        ],
        compiler_params=PARAMS,
        cost_estimate=cost(4 * positions * channels * up.shape[2], positions * up.shape[2]),
        name="conv_rest",
    )(place, near, far, before, taps, gain, shift, up, b_up, down)


def more(b, place, x, before, part, last=None, rows=0):
    positions, channels = x.shape
    args = [place, x, before] + list(part) + list(last or ())
    kind = ("packed", "halves", "plain")[0 if len(part) == 1 else 1 if part[0].dtype == part[1].dtype else 2]
    hidden = part[0].shape[1]
    scratch = []
    if last is None:
        shape = jax.ShapeDtypeStruct((positions, channels), jnp.float32)
    else:
        shape = jax.ShapeDtypeStruct((rows, positions // rows, channels), jnp.bfloat16)
        scratch.append(pltpu.VMEM((positions, channels), jnp.float32))
    if kind == "halves":
        scratch.append(pltpu.VMEM((channels, hidden), jnp.bfloat16))
    return pl.pallas_call(
        functools.partial(more_kernel, b, kind, last is not None),
        out_shape=shape,
        in_specs=[SMEM] + [VMEM] * (len(args) - 1),
        out_specs=VMEM,
        scratch_shapes=scratch,
        compiler_params=PARAMS,
        cost_estimate=cost(4 * positions * channels * hidden, positions * hidden),
        name="more" if last is None else "more_last",
    )(*args)


def halo(block, reach, odd):
    rows, count = block.shape[0], lax.axis_size("row")
    first, final = 0, rows - reach
    within = [(i, i ^ 1) for i in range(count)]
    across = [(i, i + 1) for i in range(1, count - 1, 2)]
    across += [(target, source) for source, target in across]
    pick = lambda start: lax.dynamic_slice_in_dim(block, start, reach, 0)
    far = lax.ppermute(pick(jnp.where(odd == 1, final, first)), "row", across)
    near = lax.ppermute(pick(jnp.where(odd == 1, first, final)), "row", within)
    return near, far


def after(array, *earlier):
    return lax.optimization_barrier((array, *earlier))[0]


def quarter(w_up, b_up, w_down):
    hidden = w_up.shape[1] // 2
    start = lax.rem(lax.axis_index("row"), 2) * hidden
    up = lax.dynamic_slice_in_dim(w_up, start, hidden, 1)
    down = lax.dynamic_slice_in_dim(w_down, start, hidden, 0)
    bias = lax.dynamic_slice_in_dim(b_up, start, hidden, 0)
    high = lax.reduce_precision(bias, 8, 7)
    bias = jnp.pad(jnp.stack([high, bias - high]).astype(jnp.bfloat16), ((0, MARGIN - 2), (0, 0)))
    return up, jnp.concatenate([down, bias])


def swap_hid(array):
    return lax.ppermute(array, "hid", [(0, 1), (1, 0)])


def swap_row(array, bit):
    return lax.ppermute(array, "row", [(i, i ^ bit) for i in range(lax.axis_size("row"))])


def gather(w_up, b_up, w_down):
    number, me = lax.axis_size("hid"), lax.axis_index("hid")
    arrays = [lax.all_gather(a, "hid") for a in (w_up, b_up.reshape(1, -1), w_down)]
    pick = lambda a, k: lax.dynamic_index_in_dim(a, lax.rem(me + k, number), 0, keepdims=False)
    return [tuple(pick(a, k) for a in arrays) for k in range(1, number)]


def shards(features, dw_weight, dw_bias, ln_gain, ln_bias, w_up, b_up, w_down, b_down, layer_scale):
    blocks, reach = dw_weight.shape[0], dw_weight.shape[1] // 2
    rows, columns, channels = features.shape
    number, me = lax.axis_size("hid"), lax.axis_index("hid")
    row, count = lax.axis_index("row"), lax.axis_size("row")
    odd, high = lax.rem(row, 2), lax.rem(row // 4, 2)
    width = columns // number
    pairs = number == 2 and w_up.shape[2] == 2 * channels and count % 8 == 0

    def window(b):
        extra = MARGIN * (blocks - 1 - b)
        size = min(columns, width + (extra if number == 2 else 2 * extra))
        return jnp.clip(me * width - extra, 0, columns - size), size

    state, start = features, 0
    fetched = None
    for b in range(blocks):
        to, size = window(b)
        if b == 0:
            from_halo = to
            near, far = halo(lax.dynamic_slice_in_dim(state, to, size, 1), reach, odd)
        else:
            from_halo = start
            near, far = halo(state, reach, odd)
        place = jnp.stack([to - start, from_halo - to + MARGIN, odd, high]).astype(jnp.int32)
        before = conv_own(b, place, state, size, dw_weight, dw_bias)
        if pairs and b == 0:
            up, down = quarter(w_up[b], b_up[b], w_down[b])
            mine = swap_hid(lax.dynamic_slice_in_dim(up, high * (channels // 2), channels // 2, 0))
            down = swap_hid(down)
            mine = after(mine, before)
            other = swap_row(mine, 4)
            before = after(before, mine)
        normed, total = conv_rest(
            b, place, near, far, before, dw_weight, ln_gain, ln_bias, w_up, b_up, w_down
        )
        if not pairs:
            parts = gather(w_up[b], b_up[b], w_down[b])
        elif b == 0:
            down = after(down, total)
            parts = [(mine, other, down), tuple(swap_row(a, 1) for a in (mine, other, down))]
            if blocks > 1:
                fetched = swap_hid(after(jnp.concatenate(quarter(w_up[1], b_up[1], w_down[1])), down))
        else:
            fetched = after(fetched, total)
            parts = [(fetched,), (swap_row(fetched, 1),)]
            if b + 1 < blocks:
                weights = (w_up[b + 1], b_up[b + 1], w_down[b + 1])
                fetched = swap_hid(after(jnp.concatenate(quarter(*weights)), fetched))
        ending = (state, b_down, layer_scale)
        for k, part in enumerate(parts):
            last = ending if k == len(parts) - 1 else None
            total = more(b, place, normed, total, part, last, rows)
        state, start = total, to
    if number == 2:
        other = swap_hid(state)
        left, right = jnp.where(me == 0, state, other), jnp.where(me == 0, other, state)
        return jnp.concatenate([left, right], axis=1)
    return lax.all_gather(state, "hid", axis=1, tiled=True)


def solution(mesh):
    return jax.shard_map(
        shards,
        mesh=mesh,
        in_specs=(
            P("row", None, None),
            P(),
            P(),
            P(),
            P(),
            P(None, None, "hid"),
            P(None, "hid"),
            P(None, "hid", None),
            P(),
            P(),
        ),
        out_specs=P("row", None, None),
        check_vma=False,
    )
```

```python
import functools

import jax
import jax.numpy as jnp
from jax import lax
from jax.experimental import pallas as pl
from jax.experimental.pallas import tpu as pltpu
from jax.sharding import PartitionSpec as P

LANES = 128
MARGIN = 16
LONG = 10**11
ERF = (
    0.7978842161099958,
    0.03633428353366734,
    -3.3130008237205104e-05,
    -5.524015421773868e-05,
    3.969108888631555e-06,
    -1.33446374821295e-07,
    1.8056156531812635e-09,
)
VMEM = pl.BlockSpec(memory_space=pltpu.VMEM)
SMEM = pl.BlockSpec(memory_space=pltpu.SMEM)
HBM = pl.BlockSpec(memory_space=pltpu.HBM)
PARAMS = pltpu.CompilerParams(vmem_limit_bytes=20 * 1024 * 1024)
COPIES = pltpu.CompilerParams(vmem_limit_bytes=60 * 1024 * 1024)


def gelu(u):
    v = u * u
    p = jnp.full_like(u, ERF[-1])
    for c in ERF[-2::-1]:
        p = p * v + c
    half = 0.5 * u
    return half * jnp.tanh(u * p) + half


def tile_of(width):
    return next(s for s in (48, 32, 16) if width % s == 0)


def row_of(place, d, rows):
    return jnp.where(place[4] * place[2] == 1, rows - 1 - d, d)


def tap_of(place, t, size):
    return jnp.where(place[2] == 1, size - 1 - t, t)


def convolve(b, place, sums, wide, inputs, outputs, taps, c, lanes, start, step):
    size = taps.shape[1]
    reach = size // 2
    for i, position in enumerate(inputs):
        used = [(n, position - d + reach) for n, d in enumerate(outputs)]
        used = [(n, tap_of(place, t, size)) for n, t in used if 0 <= t < size]
        if not used:
            continue
        for j in range(size):
            first = start + MARGIN + j - reach
            x = wide[c, i, first : first + step]
            for n, t in used:
                sums[n] = sums[n] + x * taps[b, t, j : j + 1, lanes]
    return sums


def own_kernel(b, place, own, near, taps, bias, out, wide):
    groups, rows, width, _ = out.shape
    reach = near.shape[0]
    fill_own(place, own, wide, rows)
    back = place[2] if b == 0 else 1
    sources = [(near, jnp.where(back == 1, reach - 1 - k, k)) for k in range(reach)]
    fill_halo(place, sources, wide, rows)
    step = tile_of(width)
    outputs = range(rows)
    inputs = range(rows + reach)

    def group(c, _):
        lanes = pl.ds(pl.multiple_of(c * LANES, LANES), LANES)
        for start in range(0, width, step):
            sums = [jnp.broadcast_to(bias[b : b + 1, lanes], (step, LANES)) for _ in range(rows)]
            sums = convolve(b, place, sums, wide, inputs, outputs, taps, c, lanes, start, step)
            for d in range(rows):
                out[c, d, start : start + step] = sums[d]
        return 0

    lax.fori_loop(0, groups, group, 0)


def fill_own(place, own, wide, rows):
    groups, _, columns, _ = wide.shape
    for k in range(columns // MARGIN):
        at = place[0] + (k - 1) * MARGIN
        inside = (at >= 0) & (at <= own.shape[1] - MARGIN)
        at = pl.multiple_of(jnp.clip(at, 0, own.shape[1] - MARGIN), MARGIN)
        for d in range(rows):
            for c in range(groups):
                x = own[row_of(place, d, rows), pl.ds(at, MARGIN), c * LANES : (c + 1) * LANES]
                x = jnp.where(inside, x.astype(jnp.float32), 0.0)
                wide[c, d, k * MARGIN : (k + 1) * MARGIN] = x


def fill_halo(place, sources, wide, first):
    groups, _, columns, _ = wide.shape
    size = sources[0][0].shape[1]
    at = pl.ds(pl.multiple_of(place[1], 8), size)
    for i, (ref, row) in enumerate(sources):
        for c in range(groups):
            zeros = jnp.zeros((2 * MARGIN, LANES), jnp.float32)
            wide[c, first + i, : 2 * MARGIN] = zeros
            wide[c, first + i, columns - 2 * MARGIN :] = zeros
            x = ref[row, :, c * LANES : (c + 1) * LANES].astype(jnp.float32)
            wide[c, first + i, at] = x


def add_far(b, place, chosen, far, before, taps, conv, wide):
    groups, _, width, _ = before.shape
    reach = taps.shape[1] // 2
    rows = [(ref, k) for ref in far for k in range(ref.shape[0])]
    if b == 0:
        rows = [(far[0], jnp.where(place[2] == 1, k, reach - 1 - k)) for k in range(reach)]
    rows = rows[: max(0, reach - min(chosen))]
    inputs = [-1 - k for k in range(len(rows))]
    fill_halo(place, rows, wide, 0)
    step = tile_of(width)

    def group(c, _):
        lanes = pl.ds(pl.multiple_of(c * LANES, LANES), LANES)
        for start in range(0, width, step):
            sums = [before[c, d, start : start + step] for d in chosen]
            sums = convolve(b, place, sums, wide, inputs, chosen, taps, c, lanes, start, step)
            for n in range(len(chosen)):
                conv[c, n, start : start + step] = sums[n]
        return 0

    lax.fori_loop(0, groups, group, 0)


def normalise(b, conv, gain, shift, out):
    groups, rows, width, _ = conv.shape
    channels = groups * LANES
    for r in range(rows):
        x = [conv[c, r].astype(jnp.bfloat16).astype(jnp.float32) for c in range(groups)]
        mean = jnp.sum(functools.reduce(jnp.add, x), axis=1, keepdims=True) * (1.0 / channels)
        x = [v - mean for v in x]
        var = jnp.sum(functools.reduce(jnp.add, [v * v for v in x]), axis=1, keepdims=True)
        scale = lax.rsqrt(var * (1.0 / channels) + 1e-06)
        for c in range(groups):
            lanes = slice(c * LANES, (c + 1) * LANES)
            y = x[c] * scale * gain[b : b + 1, lanes] + shift[b : b + 1, lanes]
            out[r * width : (r + 1) * width, lanes] = y.astype(out.dtype)


def project(x, up, b_up, down, total, before=None):
    hidden = down.shape[0]
    part = 256 if hidden % 256 == 0 else 128
    for k in range(0, hidden, part):
        u = jnp.dot(x[...], up[:, k : k + part], preferred_element_type=jnp.float32)
        h = gelu(u + b_up[:, k : k + part]).astype(jnp.bfloat16)
        y = jnp.dot(h, down[k : k + part, :], preferred_element_type=jnp.float32)
        if k:
            total[...] += y
        else:
            total[...] = y if before is None else before[...] + y


def rest_kernel(b, chosen, number, place, *refs):
    far, refs = refs[:number], refs[number:]
    before, taps, gain, shift, up, b_up, down, normed, total, conv, wide = refs
    add_far(b, place, chosen, far, before, taps, conv, wide)
    normalise(b, conv, gain, shift, normed)
    project(normed, up.at[b], b_up.at[b : b + 1], down.at[b], total)


def more_kernel(b, chosen, kind, number, final, place, x, before, *refs):
    channels = x.shape[1]
    refs = list(refs)
    parts = [refs.pop(0) for _ in range(number)]
    state, b_down, scale = (refs.pop(0) for _ in range(3))
    out = refs.pop(0)
    sends = [] if final else [refs.pop(0) for _ in range(2)]
    total = refs.pop(0)
    odd, parity = place[2], place[3]
    pieces = []
    if kind == "plain":
        pieces = [(parts[n], parts[n + 1][...], parts[n + 2]) for n in range(0, number, 3)]
    else:
        if kind == "joined":
            views = [(p.at[:channels], p.at[channels : p.shape[0] - MARGIN], p.at[p.shape[0] - MARGIN :]) for p in parts]
        else:
            views = [(p.at[:channels], q, p.at[channels:]) for p, q in zip(parts[::2], parts[1::2])]
        for up, down, bias in views:
            terms = bias[...].astype(jnp.float32)
            pieces.append((up, terms[0:1] + terms[1:2], down))
    first = before
    for piece in pieces:
        project(x, *piece, total, first)
        first = total
    count, width, _ = out.shape
    rows = state.shape[0]
    for n, d in enumerate(chosen):
        at = pl.ds(pl.multiple_of(place[0], MARGIN), width)
        s = state[row_of(place, d, rows), at, :].astype(jnp.float32)
        y = first[n * width : (n + 1) * width, :] + b_down[b : b + 1]
        s = s + scale[b : b + 1] * y
        if final:
            out[jnp.where(odd == 1, count - 1 - n, n)] = s.astype(out.dtype)
            continue
        out[n] = s.astype(out.dtype)
        total[n * width : (n + 1) * width, :] = s
        far, near = sends
        size = near.shape[1]
        s = total[pl.ds(pl.multiple_of(n * width + place[5], 8), size), :].astype(out.dtype)
        reach = near.shape[0]
        if d < reach:
            far[d] = s
        if d >= rows - reach:
            near[d - (rows - reach)] = s


def take(b, place, weights, parts, up, down, bias, terms):
    w_up, b_up, w_down = weights
    hidden = w_up.shape[2] // parts
    at = place[2] * (w_up.shape[2] // 2) + (place[3] * hidden if parts == 4 else 0)
    at = pl.ds(pl.multiple_of(at, hidden), hidden)
    value = b_up[b : b + 1, at]
    high = value.astype(jnp.bfloat16).astype(jnp.float32)
    low = (value - high).astype(jnp.bfloat16).astype(jnp.float32)
    row = lax.broadcasted_iota(jnp.int32, (MARGIN, hidden), 0)
    terms[...] = jnp.where(row == 0, high, jnp.where(row == 1, low, 0.0)).astype(terms.dtype)
    return [(w_up.at[b, :, at], up), (w_down.at[b, at, :], down), (terms, bias)]


def carry(copies, sems):
    copies = [pltpu.make_async_copy(*copy, sems.at[n]) for n, copy in enumerate(copies)]
    for copy in copies:
        copy.start()
    for copy in copies:
        copy.wait()


def prepare_kernel(place, features, *refs):
    weights, refs = refs[: 3 if len(refs) > 3 else 0], refs[3 if len(refs) > 3 else 0 :]
    outer, inner, *refs = refs
    reach, size, _ = outer.shape
    last = features.shape[0] - reach
    at = pl.ds(pl.multiple_of(place[6], MARGIN), size)
    copies = [
        (features.at[pl.ds(place[2] * last, reach), at], outer),
        (features.at[pl.ds((1 - place[2]) * last, reach), at], inner),
    ]
    if weights:
        up, down, terms, _ = refs
        channels = features.shape[2]
        copies += take(0, place, weights, 4, up.at[:channels], down, up.at[channels:], terms)
    carry(copies, refs[-1])


def pack_kernel(b, place, w_up, b_up, w_down, out, terms, sems):
    channels, last = w_up.shape[1], out.shape[0] - MARGIN
    outs = out.at[:channels], out.at[channels:last], out.at[last:]
    carry(take(b, place, (w_up, b_up, w_down), 2, *outs, terms), sems)


def cost(flops):
    return pl.CostEstimate(flops=flops, bytes_accessed=0, transcendentals=0)


def prepare(place, features, reach, size, weights=()):
    channels = features.shape[2]
    shapes = [jax.ShapeDtypeStruct((reach, size, channels), jnp.bfloat16)] * 2
    scratch = [pltpu.SemaphoreType.DMA((5,))]
    if weights:
        hidden = weights[0].shape[2] // 4
        sizes = [(channels + MARGIN, hidden), (hidden, channels)]
        shapes += [jax.ShapeDtypeStruct(size, jnp.bfloat16) for size in sizes]
        scratch.insert(0, pltpu.VMEM((MARGIN, hidden), jnp.bfloat16))
    return pl.pallas_call(
        prepare_kernel,
        out_shape=shapes,
        in_specs=[SMEM, HBM] + ([HBM, VMEM, HBM] if weights else []),
        out_specs=[VMEM] * len(shapes),
        scratch_shapes=scratch,
        compiler_params=COPIES,
        cost_estimate=cost(1),
        name="prepare",
    )(place, features, *weights)


def pack(b, place, weights):
    _, channels, hidden = weights[0].shape
    hidden //= 2
    shape = (channels + hidden + MARGIN, channels)
    return pl.pallas_call(
        functools.partial(pack_kernel, b),
        out_shape=jax.ShapeDtypeStruct(shape, jnp.bfloat16),
        in_specs=[SMEM, HBM, VMEM, HBM],
        out_specs=VMEM,
        scratch_shapes=[
            pltpu.VMEM((MARGIN, hidden), jnp.bfloat16),
            pltpu.SemaphoreType.DMA((3,)),
        ],
        compiler_params=PARAMS,
        cost_estimate=cost(1),
        name="pack",
    )(place, *weights)


def conv_own(b, place, own, near, width, taps, bias):
    rows, _, channels = own.shape
    groups, reach = channels // LANES, near.shape[0]
    return pl.pallas_call(
        functools.partial(own_kernel, b),
        out_shape=jax.ShapeDtypeStruct((groups, rows, width, LANES), jnp.float32),
        in_specs=[SMEM] + [VMEM] * 4,
        out_specs=VMEM,
        scratch_shapes=[
            pltpu.VMEM((groups, rows + reach, width + 2 * MARGIN, LANES), jnp.float32)
        ],
        compiler_params=PARAMS,
        cost_estimate=cost(1),
        name="conv_own",
    )(place, own, near, taps, bias)


def conv_rest(b, chosen, place, far, before, taps, gain, shift, up, b_up, down):
    groups, _, width, _ = before.shape
    channels, reach = groups * LANES, taps.shape[1] // 2
    positions = len(chosen) * width
    args = [place, *far, before, taps, gain, shift, up, b_up, down]
    return pl.pallas_call(
        functools.partial(rest_kernel, b, chosen, len(far)),
        out_shape=(
            jax.ShapeDtypeStruct((positions, channels), jnp.bfloat16),
            jax.ShapeDtypeStruct((positions, channels), jnp.float32),
        ),
        in_specs=[SMEM] + [VMEM] * (len(args) - 1),
        out_specs=(VMEM, VMEM),
        scratch_shapes=[
            pltpu.VMEM((groups, len(chosen), width, LANES), jnp.float32),
            pltpu.VMEM((groups, reach, width + 2 * MARGIN, LANES), jnp.float32),
        ],
        compiler_params=PARAMS,
        cost_estimate=cost(LONG if min(chosen) else 1),
        name="conv_rest",
    )(*args)


def more(b, chosen, place, x, before, kind, parts, state, b_down, scale, halo_shape):
    positions, channels = x.shape
    final = halo_shape is None
    args = [place, x, before, *parts, state, b_down, scale]
    shapes = [(len(chosen), positions // len(chosen), channels)]
    if not final:
        reach, size = halo_shape
        shapes += [(reach, size, channels)] * 2
    return pl.pallas_call(
        functools.partial(more_kernel, b, chosen, kind, len(parts), final),
        out_shape=[jax.ShapeDtypeStruct(shape, jnp.bfloat16) for shape in shapes],
        in_specs=[SMEM] + [VMEM] * (len(args) - 1),
        out_specs=[VMEM] * len(shapes),
        scratch_shapes=[pltpu.VMEM((positions, channels), jnp.float32)],
        compiler_params=PARAMS,
        cost_estimate=cost(1),
        name="more",
    )(*args)


def within(array):
    return lax.ppermute(array, "row", [(i, i ^ 1) for i in range(lax.axis_size("row"))])


def across(array):
    pairs = [(i, i + 1) for i in range(1, lax.axis_size("row") - 1, 2)]
    return lax.ppermute(array, "row", pairs + [(target, source) for source, target in pairs])


def swap_hid(array):
    return lax.ppermute(array, "hid", [(0, 1), (1, 0)])


def swap_row(array, bit):
    return lax.ppermute(array, "row", [(i, i ^ bit) for i in range(lax.axis_size("row"))])


def after(array, *earlier):
    return lax.optimization_barrier((array, *earlier))[0]


def gather(w_up, b_up, w_down):
    number, me = lax.axis_size("hid"), lax.axis_index("hid")
    arrays = [lax.all_gather(a, "hid") for a in (w_up, b_up.reshape(1, -1), w_down)]
    pick = lambda a, k: lax.dynamic_index_in_dim(a, lax.rem(me + k, number), 0, keepdims=False)
    return [pick(a, k) for k in range(1, number) for a in arrays]


def shards(features, dw_weight, dw_bias, ln_gain, ln_bias, w_up, b_up, w_down, b_down, layer_scale):
    blocks, reach = dw_weight.shape[0], dw_weight.shape[1] // 2
    rows, columns, channels = features.shape
    number, me = lax.axis_size("hid"), lax.axis_index("hid")
    row, count = lax.axis_index("row"), lax.axis_size("row")
    odd, parity = lax.rem(row, 2), lax.rem(row // 4, 2)
    width = columns // number
    pairs = number == 2 and w_up.shape[2] == 2 * channels and count % 8 == 0

    def window(reach, unit):
        extra = -(-reach // unit) * unit
        size = min(columns, width + (extra if number == 2 else 2 * extra))
        return jnp.clip(me * width - extra, 0, columns - size), size

    def edge(b):
        return window(reach * (blocks - b), 8 if b else MARGIN)

    def place_of(b):
        to, _ = window(reach * (blocks - 1 - b), MARGIN)
        start = window(reach * (blocks - b), MARGIN)[0] if b else 0
        halo, _ = edge(b)
        later, _ = edge(b + 1)
        values = [to - start, halo - to + MARGIN, odd, parity, int(b == 0), later - to, halo]
        return jnp.stack([jnp.int32(v) for v in values])

    places = [place_of(b) for b in range(blocks)]
    everything = tuple(range(rows))
    weights = (w_up, b_up, w_down)

    outer, inner, *first = prepare(
        places[0], features, reach, edge(0)[1], weights if pairs else ()
    )
    far, near = [across(outer)], within(inner)
    state = features
    if pairs:
        up, down = swap_hid(first[0]), swap_hid(first[1])
    for b in range(blocks):
        place, final = places[b], b == blocks - 1
        _, size = window(reach * (blocks - 1 - b), MARGIN)
        before = conv_own(b, place, state, near, size, dw_weight, dw_bias)
        rest = lambda chosen, far, before: conv_rest(
            b, chosen, place, far, before, dw_weight, ln_gain, ln_bias, *weights
        )
        add = lambda chosen, work, parts: more(
            b, chosen, place, *work, kind, parts, state, b_down, layer_scale,
            None if final else (reach, edge(b + 1)[1]),
        )
        if pairs and not final:
            later = swap_hid(pack(b + 1, places[b + 1], weights))
        if pairs and b == 0:
            up = after(up, before)
            up_other, down_other = swap_row(up, 4), swap_row(down, 4)
        elif pairs:
            joined = after(joined, before)
            kind, parts = "joined", [joined, within(joined)]
        halves = (everything[rows // 2 :], everything[: rows // 2]) if final else (everything,)
        work = [rest(chosen, far, before) for chosen in halves]
        if pairs and b == 0:
            up_other, down_other = (after(a, work[0][1]) for a in (up_other, down_other))
            parts = [up, down, up_other, down_other]
            kind, parts = "pairs", parts + [within(a) for a in parts]
        elif not pairs:
            kind, parts = "plain", gather(w_up[b], b_up[b], w_down[b])
        results = [add(chosen, w, parts) for chosen, w in zip(halves, work)]
        if not final:
            state, outer, inner = results[0]
            far, near = [across(outer)], within(inner)
            if pairs:
                joined = later
    inner, outer = (r[0] for r in results)
    if number == 1:
        columns_of = lambda a: a
    elif number == 2:
        def columns_of(a):
            other = swap_hid(a)
            return jnp.concatenate(
                [jnp.where(me == 0, a, other), jnp.where(me == 0, other, a)], axis=1
            )
    else:
        columns_of = lambda a: lax.all_gather(a, "hid", axis=1, tiled=True)
    inner, outer = columns_of(inner), columns_of(outer)
    return jnp.concatenate([jnp.where(odd == 1, inner, outer), jnp.where(odd == 1, outer, inner)])


def solution(mesh):
    return jax.shard_map(
        shards,
        mesh=mesh,
        in_specs=(
            P("row", None, None),
            P(),
            P(),
            P(),
            P(),
            P(None, None, "hid"),
            P(None, "hid"),
            P(None, "hid", None),
            P(),
            P(),
        ),
        out_specs=P("row", None, None),
        check_vma=False,
    )
```

```python
import functools

import jax
import jax.numpy as jnp
from jax import lax
from jax.experimental import pallas as pl
from jax.experimental.pallas import tpu as pltpu
from jax.sharding import PartitionSpec as P

LANES = 128
MARGIN = 16
LONG = 10**11
ERF = (
    0.7978842161099958,
    0.03633428353366734,
    -3.3130008237205104e-05,
    -5.524015421773868e-05,
    3.969108888631555e-06,
    -1.33446374821295e-07,
    1.8056156531812635e-09,
)
VMEM = pl.BlockSpec(memory_space=pltpu.VMEM)
HBM = pl.BlockSpec(memory_space=pltpu.HBM)
PARAMS = pltpu.CompilerParams(vmem_limit_bytes=20 * 1024 * 1024)
COPIES = pltpu.CompilerParams(vmem_limit_bytes=60 * 1024 * 1024)


def gelu(u):
    v = u * u
    p = jnp.full_like(u, ERF[-1])
    for c in ERF[-2::-1]:
        p = p * v + c
    half = 0.5 * u
    return half * jnp.tanh(u * p) + half


def tile_of(width):
    return next(s for s in (48, 32, 16) if width % s == 0)


class Layout:
    def __init__(self, features, kernels):
        self.blocks, self.reach = kernels.shape[0], kernels.shape[1] // 2
        self.rows, self.columns, self.channels = features.shape
        self.number = lax.axis_size("hid")
        self.width = self.columns // self.number

    def size(self, reach, unit):
        extra = -(-reach // unit) * unit
        return extra, min(self.columns, self.width + (1 if self.number == 2 else 2) * extra)

    def start(self, reach, unit):
        extra, size = self.size(reach, unit)
        return jnp.clip(lax.axis_index("hid") * self.width - extra, 0, self.columns - size)

    def window(self, b):
        return self.reach * (self.blocks - 1 - b), MARGIN

    def edge(self, b):
        return self.reach * (self.blocks - b), 8 if b else MARGIN

    def place(self, b):
        to, halo = self.start(*self.window(b)), self.start(*self.edge(b))
        start = self.start(*self.window(b - 1)) if b else 0
        later = self.start(*self.edge(b + 1))
        row = lax.axis_index("row")
        odd, parity = lax.rem(row, 2), lax.rem(lax.div(row, 4), 2)
        return to - start, halo - to + MARGIN, odd, parity, int(b == 0), later - to, halo


def row_of(place, d, rows):
    return jnp.where(place[4] * place[2] == 1, rows - 1 - d, d)


def tap_of(place, t, size):
    return jnp.where(place[2] == 1, size - 1 - t, t)


def convolve(b, place, sums, wide, inputs, outputs, taps, c, lanes, start, step):
    size = taps.shape[1]
    reach = size // 2
    for i, position in enumerate(inputs):
        used = [(n, position - d + reach) for n, d in enumerate(outputs)]
        used = [(n, tap_of(place, t, size)) for n, t in used if 0 <= t < size]
        if not used:
            continue
        for j in range(size):
            first = start + MARGIN + j - reach
            x = wide[c, i, first : first + step]
            for n, t in used:
                sums[n] = sums[n] + x * taps[b, t, j : j + 1, lanes]
    return sums


def own_kernel(b, layout, own, near, taps, bias, out, wide):
    place = layout.place(b)
    groups, rows, width, _ = out.shape
    reach = near.shape[0]
    fill_own(place, own, wide, rows)
    back = place[2] if b == 0 else 1
    sources = [(near, jnp.where(back == 1, reach - 1 - k, k)) for k in range(reach)]
    fill_halo(place, sources, wide, rows)
    step = tile_of(width)
    outputs = range(rows)
    inputs = range(rows + reach)

    def group(c, _):
        lanes = pl.ds(pl.multiple_of(c * LANES, LANES), LANES)
        for start in range(0, width, step):
            sums = [jnp.broadcast_to(bias[b : b + 1, lanes], (step, LANES)) for _ in range(rows)]
            sums = convolve(b, place, sums, wide, inputs, outputs, taps, c, lanes, start, step)
            for d in range(rows):
                out[c, d, start : start + step] = sums[d]
        return 0

    lax.fori_loop(0, groups, group, 0)


def fill_own(place, own, wide, rows):
    groups, _, columns, _ = wide.shape
    for k in range(columns // MARGIN):
        at = place[0] + (k - 1) * MARGIN
        inside = (at >= 0) & (at <= own.shape[1] - MARGIN)
        at = pl.multiple_of(jnp.clip(at, 0, own.shape[1] - MARGIN), MARGIN)
        for d in range(rows):
            for c in range(groups):
                x = own[row_of(place, d, rows), pl.ds(at, MARGIN), c * LANES : (c + 1) * LANES]
                x = jnp.where(inside, x.astype(jnp.float32), 0.0)
                wide[c, d, k * MARGIN : (k + 1) * MARGIN] = x


def fill_halo(place, sources, wide, first):
    groups, _, columns, _ = wide.shape
    size = sources[0][0].shape[1]
    at = pl.ds(pl.multiple_of(place[1], 8), size)
    for i, (ref, row) in enumerate(sources):
        for c in range(groups):
            zeros = jnp.zeros((2 * MARGIN, LANES), jnp.float32)
            wide[c, first + i, : 2 * MARGIN] = zeros
            wide[c, first + i, columns - 2 * MARGIN :] = zeros
            x = ref[row, :, c * LANES : (c + 1) * LANES].astype(jnp.float32)
            wide[c, first + i, at] = x


def add_far(b, place, chosen, far, before, taps, conv, wide):
    groups, _, width, _ = before.shape
    reach = taps.shape[1] // 2
    rows = [(ref, k) for ref in far for k in range(ref.shape[0])]
    if b == 0:
        rows = [(far[0], jnp.where(place[2] == 1, k, reach - 1 - k)) for k in range(reach)]
    rows = rows[: max(0, reach - min(chosen))]
    inputs = [-1 - k for k in range(len(rows))]
    fill_halo(place, rows, wide, 0)
    step = tile_of(width)

    def group(c, _):
        lanes = pl.ds(pl.multiple_of(c * LANES, LANES), LANES)
        for start in range(0, width, step):
            sums = [before[c, d, start : start + step] for d in chosen]
            sums = convolve(b, place, sums, wide, inputs, chosen, taps, c, lanes, start, step)
            for n in range(len(chosen)):
                conv[c, n, start : start + step] = sums[n]
        return 0

    lax.fori_loop(0, groups, group, 0)


def normalise(b, conv, gain, shift, out):
    groups, rows, width, _ = conv.shape
    channels = groups * LANES
    for r in range(rows):
        x = [conv[c, r].astype(jnp.bfloat16).astype(jnp.float32) for c in range(groups)]
        mean = jnp.sum(functools.reduce(jnp.add, x), axis=1, keepdims=True) * (1.0 / channels)
        x = [v - mean for v in x]
        var = jnp.sum(functools.reduce(jnp.add, [v * v for v in x]), axis=1, keepdims=True)
        scale = lax.rsqrt(var * (1.0 / channels) + 1e-06)
        for c in range(groups):
            lanes = slice(c * LANES, (c + 1) * LANES)
            y = x[c] * scale * gain[b : b + 1, lanes] + shift[b : b + 1, lanes]
            out[r * width : (r + 1) * width, lanes] = y.astype(out.dtype)


def project(x, up, b_up, down, total, before=None):
    hidden = down.shape[0]
    part = 256 if hidden % 256 == 0 else 128
    for k in range(0, hidden, part):
        u = jnp.dot(x[...], up[:, k : k + part], preferred_element_type=jnp.float32)
        h = gelu(u + b_up[:, k : k + part]).astype(jnp.bfloat16)
        y = jnp.dot(h, down[k : k + part, :], preferred_element_type=jnp.float32)
        if k:
            total[...] += y
        else:
            total[...] = y if before is None else before[...] + y


def rest_kernel(b, layout, chosen, number, *refs):
    place = layout.place(b)
    far, refs = refs[:number], refs[number:]
    before, taps, gain, shift, up, b_up, down, normed, total, conv, wide = refs
    add_far(b, place, chosen, far, before, taps, conv, wide)
    normalise(b, conv, gain, shift, normed)
    project(normed, up.at[b], b_up.at[b : b + 1], down.at[b], total)


def more_kernel(b, layout, chosen, kind, number, final, x, before, *refs):
    place = layout.place(b)
    channels = x.shape[1]
    refs = list(refs)
    parts = [refs.pop(0) for _ in range(number)]
    state, b_down, scale = (refs.pop(0) for _ in range(3))
    out = refs.pop(0)
    sends = [] if final else [refs.pop(0) for _ in range(2)]
    total = refs.pop(0)
    odd, parity = place[2], place[3]
    pieces = []
    if kind == "plain":
        pieces = [(parts[n], parts[n + 1][...], parts[n + 2]) for n in range(0, number, 3)]
    else:
        if kind == "joined":
            views = [(p.at[:channels], p.at[channels : p.shape[0] - MARGIN], p.at[p.shape[0] - MARGIN :]) for p in parts]
        else:
            views = [(p.at[:channels], q, p.at[channels:]) for p, q in zip(parts[::2], parts[1::2])]
        for up, down, bias in views:
            terms = bias[...].astype(jnp.float32)
            pieces.append((up, terms[0:1] + terms[1:2], down))
    first = before
    for piece in pieces:
        project(x, *piece, total, first)
        first = total
    count, width, _ = out.shape
    rows = state.shape[0]
    for n, d in enumerate(chosen):
        at = pl.ds(pl.multiple_of(place[0], MARGIN), width)
        s = state[row_of(place, d, rows), at, :].astype(jnp.float32)
        y = first[n * width : (n + 1) * width, :] + b_down[b : b + 1]
        s = s + scale[b : b + 1] * y
        if final:
            out[jnp.where(odd == 1, count - 1 - n, n)] = s.astype(out.dtype)
            continue
        out[n] = s.astype(out.dtype)
        total[n * width : (n + 1) * width, :] = s
        far, near = sends
        size = near.shape[1]
        s = total[pl.ds(pl.multiple_of(n * width + place[5], 8), size), :].astype(out.dtype)
        reach = near.shape[0]
        if d < reach:
            far[d] = s
        if d >= rows - reach:
            near[d - (rows - reach)] = s


def take(b, place, weights, parts, up, down):
    w_up, _, w_down = weights
    hidden = w_up.shape[2] // parts
    at = place[2] * (w_up.shape[2] // 2) + (place[3] * hidden if parts == 4 else 0)
    at = pl.ds(pl.multiple_of(at, hidden), hidden)
    return at, [(w_up.at[b, :, at], up), (w_down.at[b, at, :], down)]


def in_two_terms(value, terms):
    high = value.astype(jnp.bfloat16).astype(jnp.float32)
    low = (value - high).astype(jnp.bfloat16).astype(jnp.float32)
    row = lax.broadcasted_iota(jnp.int32, terms.shape, 0)
    terms[...] = jnp.where(row == 0, high, jnp.where(row == 1, low, 0.0)).astype(terms.dtype)


def start(copies, sems):
    copies = [pltpu.make_async_copy(*copy, sems.at[n]) for n, copy in enumerate(copies)]
    for copy in copies:
        copy.start()
    return copies


def prepare_kernel(layout, features, *refs):
    place = layout.place(0)
    weights, refs = refs[: 3 if len(refs) > 5 else 0], refs[3 if len(refs) > 5 else 0 :]
    *refs, sems = refs
    if weights:
        *refs, bias, terms = refs
    outs, stages = list(refs[: len(refs) // 2]), list(refs[len(refs) // 2 :])
    reach, size, _ = outs[0].shape
    last = layout.rows - reach
    at = pl.ds(pl.multiple_of(place[6], MARGIN), size)
    sources = [
        features.at[pl.ds(place[2] * last, reach), at],
        features.at[pl.ds((1 - place[2]) * last, reach), at],
    ]
    if weights:
        channels = layout.channels
        hidden, taken = take(0, place, weights, 4, stages[2].at[:channels], stages[3])
        first = start([*taken, (weights[1], bias)], sems.at[0])
        rest = start(list(zip(sources, stages)), sems.at[1])
        first[2].wait()
        in_two_terms(bias[0:1, hidden], terms)
        first[0].wait()
        legs = [(stages[2].at[:channels], outs[2].at[:channels]), (terms, outs[2].at[channels:])]
        legs = start(legs, sems.at[2])
        first[1].wait()
        legs += start([(stages[3], outs[3])], sems.at[3])
    else:
        rest = start(list(zip(sources, stages)), sems.at[1])
        legs = []
    for n, copy in enumerate(rest):
        copy.wait()
        legs += start([(stages[n], outs[n])], sems.at[4 + n])
    for copy in legs:
        copy.wait()


def pack_kernel(b, layout, w_up, b_up, w_down, out, terms, sems):
    channels, last = layout.channels, out.shape[0] - MARGIN
    outs = out.at[:channels], out.at[channels:last]
    hidden, copies = take(b, layout.place(b), (w_up, b_up, w_down), 2, *outs)
    copies = start(copies, sems.at[0])
    in_two_terms(b_up[b : b + 1, hidden], terms)
    copies += start([(terms, out.at[last:])], sems.at[1])
    for copy in copies:
        copy.wait()


def cost(flops):
    return pl.CostEstimate(flops=flops, bytes_accessed=0, transcendentals=0)


def prepare(layout, features, weights=()):
    _, size = layout.size(*layout.edge(0))
    channels = layout.channels
    shapes = [(layout.reach, size, channels)] * 2
    scratch = [pltpu.SemaphoreType.DMA((6, 3))]
    if weights:
        hidden = weights[0].shape[2] // 4
        shapes += [(channels + MARGIN, hidden), (hidden, channels)]
        scratch.insert(0, pltpu.VMEM((MARGIN, hidden), jnp.bfloat16))
        scratch.insert(0, pltpu.VMEM(weights[1].shape, jnp.float32))
    return pl.pallas_call(
        functools.partial(prepare_kernel, layout),
        out_shape=[jax.ShapeDtypeStruct(shape, jnp.bfloat16) for shape in shapes],
        in_specs=[HBM] + [HBM] * len(weights),
        out_specs=[HBM] * len(shapes),
        scratch_shapes=[pltpu.VMEM(shape, jnp.bfloat16) for shape in shapes] + scratch,
        compiler_params=COPIES,
        cost_estimate=cost(1),
        name="prepare",
    )(features, *weights)


def pack(b, layout, weights):
    _, channels, hidden = weights[0].shape
    hidden //= 2
    shape = (channels + hidden + MARGIN, channels)
    return pl.pallas_call(
        functools.partial(pack_kernel, b, layout),
        out_shape=jax.ShapeDtypeStruct(shape, jnp.bfloat16),
        in_specs=[HBM, VMEM, HBM],
        out_specs=VMEM,
        scratch_shapes=[
            pltpu.VMEM((MARGIN, hidden), jnp.bfloat16),
            pltpu.SemaphoreType.DMA((2, 2)),
        ],
        compiler_params=PARAMS,
        cost_estimate=cost(1),
        name="pack",
    )(*weights)


def conv_own(b, layout, own, near, width, taps, bias):
    rows, _, channels = own.shape
    groups, reach = channels // LANES, near.shape[0]
    return pl.pallas_call(
        functools.partial(own_kernel, b, layout),
        out_shape=jax.ShapeDtypeStruct((groups, rows, width, LANES), jnp.float32),
        in_specs=[VMEM] * 4,
        out_specs=VMEM,
        scratch_shapes=[
            pltpu.VMEM((groups, rows + reach, width + 2 * MARGIN, LANES), jnp.float32)
        ],
        compiler_params=PARAMS,
        cost_estimate=cost(1),
        name="conv_own",
    )(own, near, taps, bias)


def conv_rest(b, layout, chosen, far, before, taps, gain, shift, up, b_up, down):
    groups, _, width, _ = before.shape
    channels, reach = groups * LANES, taps.shape[1] // 2
    positions = len(chosen) * width
    args = [*far, before, taps, gain, shift, up, b_up, down]
    return pl.pallas_call(
        functools.partial(rest_kernel, b, layout, chosen, len(far)),
        out_shape=(
            jax.ShapeDtypeStruct((positions, channels), jnp.bfloat16),
            jax.ShapeDtypeStruct((positions, channels), jnp.float32),
        ),
        in_specs=[VMEM] * len(args),
        out_specs=(VMEM, VMEM),
        scratch_shapes=[
            pltpu.VMEM((groups, len(chosen), width, LANES), jnp.float32),
            pltpu.VMEM((groups, reach, width + 2 * MARGIN, LANES), jnp.float32),
        ],
        compiler_params=PARAMS,
        cost_estimate=cost(LONG if min(chosen) else 1),
        name="conv_rest",
    )(*args)


def more(b, layout, chosen, x, before, kind, parts, state, b_down, scale, halo_shape):
    positions, channels = x.shape
    final = halo_shape is None
    args = [x, before, *parts, state, b_down, scale]
    shapes = [(len(chosen), positions // len(chosen), channels)]
    if not final:
        reach, size = halo_shape
        shapes += [(reach, size, channels)] * 2
    return pl.pallas_call(
        functools.partial(more_kernel, b, layout, chosen, kind, len(parts), final),
        out_shape=[jax.ShapeDtypeStruct(shape, jnp.bfloat16) for shape in shapes],
        in_specs=[VMEM] * len(args),
        out_specs=[VMEM] * len(shapes),
        scratch_shapes=[pltpu.VMEM((positions, channels), jnp.float32)],
        compiler_params=PARAMS,
        cost_estimate=cost(1),
        name="more",
    )(*args)


def within(array):
    return lax.ppermute(array, "row", [(i, i ^ 1) for i in range(lax.axis_size("row"))])


def across(array):
    pairs = [(i, i + 1) for i in range(1, lax.axis_size("row") - 1, 2)]
    return lax.ppermute(array, "row", pairs + [(target, source) for source, target in pairs])


def swap_hid(array):
    return lax.ppermute(array, "hid", [(0, 1), (1, 0)])


def swap_row(array, bit):
    return lax.ppermute(array, "row", [(i, i ^ bit) for i in range(lax.axis_size("row"))])


def after(array, *earlier):
    return lax.optimization_barrier((array, *earlier))[0]


def gather(w_up, b_up, w_down):
    number, me = lax.axis_size("hid"), lax.axis_index("hid")
    arrays = [lax.all_gather(a, "hid") for a in (w_up, b_up.reshape(1, -1), w_down)]
    pick = lambda a, k: lax.dynamic_index_in_dim(a, lax.rem(me + k, number), 0, keepdims=False)
    return [pick(a, k) for k in range(1, number) for a in arrays]


def shards(features, dw_weight, dw_bias, ln_gain, ln_bias, w_up, b_up, w_down, b_down, layer_scale):
    layout = Layout(features, dw_weight)
    blocks, rows, number = layout.blocks, layout.rows, layout.number
    me, row, count = lax.axis_index("hid"), lax.axis_index("row"), lax.axis_size("row")
    odd = lax.rem(row, 2)
    pairs = number == 2 and w_up.shape[2] == 2 * layout.channels and count % 8 == 0
    everything = tuple(range(rows))
    weights = (w_up, b_up, w_down)

    outer, inner, *packed = prepare(layout, features, weights if pairs else ())
    far, near = [across(outer)], within(inner)
    state = features
    if pairs:
        up, down = swap_hid(packed[0]), swap_hid(packed[1])
    for b in range(blocks):
        final = b == blocks - 1
        _, size = layout.size(*layout.window(b))
        before = conv_own(b, layout, state, near, size, dw_weight, dw_bias)
        rest = lambda chosen, far, before: conv_rest(
            b, layout, chosen, far, before, dw_weight, ln_gain, ln_bias, *weights
        )
        add = lambda chosen, work, parts: more(
            b, layout, chosen, *work, kind, parts, state, b_down, layer_scale,
            None if final else (layout.reach, layout.size(*layout.edge(b + 1))[1]),
        )
        if pairs and not final:
            later = swap_hid(pack(b + 1, layout, weights))
        if pairs and b == 0:
            down = after(down, before)
            up_other, down_other = swap_row(up, 4), swap_row(down, 4)
        elif pairs:
            joined = after(joined, before)
            kind, parts = "joined", [joined, within(joined)]
        halves = (everything[rows // 2 :], everything[: rows // 2]) if final else (everything,)
        work = [rest(chosen, far, before) for chosen in halves]
        if pairs and b == 0:
            up_other, down_other = (after(a, work[0][1]) for a in (up_other, down_other))
            parts = [up, down, up_other, down_other]
            kind, parts = "pairs", parts + [within(a) for a in parts]
        elif not pairs:
            kind, parts = "plain", gather(w_up[b], b_up[b], w_down[b])
        results = [add(chosen, w, parts) for chosen, w in zip(halves, work)]
        if not final:
            state, outer, inner = results[0]
            far, near = [across(outer)], within(inner)
            if pairs:
                joined = later
    inner, outer = (r[0] for r in results)
    if number == 2:
        def columns_of(a):
            other = swap_hid(a)
            left, right = jnp.where(me == 0, a, other), jnp.where(me == 0, other, a)
            return jnp.concatenate([left, right], axis=1)
    elif number == 1:
        columns_of = lambda a: a
    else:
        columns_of = lambda a: lax.all_gather(a, "hid", axis=1, tiled=True)
    inner, outer = columns_of(inner), columns_of(outer)
    return jnp.concatenate([jnp.where(odd == 1, inner, outer), jnp.where(odd == 1, outer, inner)])


def solution(mesh):
    return jax.shard_map(
        shards,
        mesh=mesh,
        in_specs=(
            P("row", None, None),
            P(),
            P(),
            P(),
            P(),
            P(None, None, "hid"),
            P(None, "hid"),
            P(None, "hid", None),
            P(),
            P(),
        ),
        out_specs=P("row", None, None),
        check_vma=False,
    )
```

```python
import functools

import jax
import jax.numpy as jnp
from jax import lax
from jax.experimental import pallas as pl
from jax.experimental.pallas import tpu as pltpu
from jax.sharding import PartitionSpec as P

LANES = 128
MARGIN = 16
LONG = 10**11
ERF = (
    0.7978275766866006,
    0.036469930744144466,
    -0.00012547620415072412,
    -3.0467196783772113e-05,
    1.1126315774795922e-06,
)
VMEM = pl.BlockSpec(memory_space=pltpu.VMEM)
HBM = pl.BlockSpec(memory_space=pltpu.HBM)
PARAMS = pltpu.CompilerParams(vmem_limit_bytes=20 * 1024 * 1024)
COPIES = pltpu.CompilerParams(vmem_limit_bytes=60 * 1024 * 1024)


def twice_gelu(u):
    v = u * u
    p = jnp.full_like(u, ERF[-1])
    for c in ERF[-2::-1]:
        p = p * v + c
    return u + u * jnp.tanh(u * p)


def tile_of(width):
    return next(s for s in (48, 32, 16) if width % s == 0)


class Layout:
    def __init__(self, features, kernels):
        self.blocks, self.reach = kernels.shape[0], kernels.shape[1] // 2
        self.rows, self.columns, self.channels = features.shape
        self.number = lax.axis_size("hid")
        self.width = self.columns // self.number

    def size(self, reach, unit):
        extra = -(-reach // unit) * unit
        return extra, min(self.columns, self.width + (1 if self.number == 2 else 2) * extra)

    def start(self, reach, unit):
        extra, size = self.size(reach, unit)
        return jnp.clip(lax.axis_index("hid") * self.width - extra, 0, self.columns - size)

    def window(self, b):
        return self.reach * (self.blocks - 1 - b), MARGIN

    def edge(self, b):
        return self.reach * (self.blocks - b), 8 if b else MARGIN

    def extra(self, b):
        same = self.size(*self.window(0)) == self.size(*self.edge(0))
        return int(b == 0 and self.blocks > 1 and self.rows > self.reach and same)

    def own_rows(self, b):
        return range(-self.extra(b - 1), self.rows)

    def result_rows(self, b):
        return range(-self.extra(b), self.rows)

    def far_rows(self, b):
        return range(self.extra(b - 1), self.reach + self.extra(b))

    def place(self, b):
        to, halo = self.start(*self.window(b)), self.start(*self.edge(b))
        start = self.start(*self.window(b - 1)) if b else 0
        later = self.start(*self.edge(b + 1))
        row = lax.axis_index("row")
        odd, parity = lax.rem(row, 2), lax.rem(lax.div(row, 4), 2)
        there = jnp.where(odd == 1, row < lax.axis_size("row") - 1, row > 0)
        return to - start, halo - to + MARGIN, odd, parity, there, later - to, halo


def own_row(layout, b, place, d):
    return d + layout.extra(b - 1) if b else jnp.where(place[2] == 1, layout.rows - 1 - d, d)


def far_row(layout, b, place, k):
    rows = layout.far_rows(b)
    return k - rows[0] if b else jnp.where(place[2] == 1, k, len(rows) - 1 - k)


def tap_of(place, t, size):
    return jnp.where(place[2] == 1, size - 1 - t, t)


def convolve(b, place, sums, wide, inputs, outputs, taps, c, lanes, start, step):
    size = taps.shape[1]
    reach = size // 2
    for i, position in enumerate(inputs):
        used = [(n, position - d + reach) for n, d in enumerate(outputs)]
        used = [(n, tap_of(place, t, size)) for n, t in used if 0 <= t < size]
        if not used:
            continue
        for j in range(size):
            first = start + MARGIN + j - reach
            x = wide[c, i, first : first + step]
            for n, t in used:
                sums[n] = sums[n] + x * taps[b, t, j : j + 1, lanes]
    return sums


def own_kernel(b, layout, complete, own, near, taps, bias, *refs):
    place = layout.place(b)
    out, *conv, wide = refs
    groups, _, width, _ = out.shape
    reach = near.shape[0]
    rows, outputs = layout.own_rows(b), layout.result_rows(b)
    fill_own(layout, b, place, own, wide)
    back = place[2] if b == 0 else 1
    sources = [(near, jnp.where(back == 1, reach - 1 - k, k)) for k in range(reach)]
    fill_halo(place, sources, wide, len(rows))
    step = tile_of(width)
    inputs = range(rows[0], layout.rows + reach)

    def group(c, _):
        lanes = pl.ds(pl.multiple_of(c * LANES, LANES), LANES)
        for start in range(0, width, step):
            sums = [jnp.broadcast_to(bias[b : b + 1, lanes], (step, LANES)) for _ in outputs]
            sums = convolve(b, place, sums, wide, inputs, outputs, taps, c, lanes, start, step)
            for n, d in enumerate(outputs):
                if d in complete:
                    conv[0][c, d - complete[0], start : start + step] = sums[n]
                else:
                    out[c, n, start : start + step] = sums[n]
        return 0

    lax.fori_loop(0, groups, group, 0)


def fill_own(layout, b, place, own, wide):
    groups, _, columns, _ = wide.shape
    for k in range(columns // MARGIN):
        at = place[0] + (k - 1) * MARGIN
        inside = (at >= 0) & (at <= own.shape[1] - MARGIN)
        at = pl.multiple_of(jnp.clip(at, 0, own.shape[1] - MARGIN), MARGIN)
        for n, d in enumerate(layout.own_rows(b)):
            for c in range(groups):
                x = own[own_row(layout, b, place, d), pl.ds(at, MARGIN), c * LANES : (c + 1) * LANES]
                x = jnp.where(inside, x.astype(jnp.float32), 0.0)
                wide[c, n, k * MARGIN : (k + 1) * MARGIN] = x


def fill_halo(place, sources, wide, first):
    groups, _, columns, _ = wide.shape
    size = sources[0][0].shape[1]
    at = pl.ds(pl.multiple_of(place[1], 8), size)
    for i, (ref, row) in enumerate(sources):
        for c in range(groups):
            zeros = jnp.zeros((2 * MARGIN, LANES), jnp.float32)
            wide[c, first + i, : 2 * MARGIN] = zeros
            wide[c, first + i, columns - 2 * MARGIN :] = zeros
            x = ref[row, :, c * LANES : (c + 1) * LANES].astype(jnp.float32)
            wide[c, first + i, at] = x


def add_far(b, layout, place, chosen, far, before, taps, conv, wide):
    groups, _, width, _ = before.shape
    rows = layout.far_rows(b)
    fill_halo(place, [(far, far_row(layout, b, place, k)) for k in rows], wide, 0)
    step = tile_of(width)
    inputs = [-1 - k for k in rows]

    def group(c, _):
        lanes = pl.ds(pl.multiple_of(c * LANES, LANES), LANES)
        for start in range(0, width, step):
            sums = [before[c, n, start : start + step] for n in range(len(chosen))]
            sums = convolve(b, place, sums, wide, inputs, chosen, taps, c, lanes, start, step)
            for n in range(len(chosen)):
                conv[c, n, start : start + step] = sums[n]
        return 0

    lax.fori_loop(0, groups, group, 0)


def normalise(b, conv, gain, shift, out):
    groups, rows, width, _ = conv.shape
    channels = groups * LANES
    for r in range(rows):
        x = [conv[c, r].astype(jnp.bfloat16).astype(jnp.float32) for c in range(groups)]
        mean = jnp.sum(functools.reduce(jnp.add, x), axis=1, keepdims=True) * (1.0 / channels)
        x = [v - mean for v in x]
        var = jnp.sum(functools.reduce(jnp.add, [v * v for v in x]), axis=1, keepdims=True)
        scale = lax.rsqrt(var * (1.0 / channels) + 1e-06)
        for c in range(groups):
            lanes = slice(c * LANES, (c + 1) * LANES)
            y = x[c] * scale * gain[b : b + 1, lanes] + shift[b : b + 1, lanes]
            out[r * width : (r + 1) * width, lanes] = y.astype(out.dtype)


def project(x, up, b_up, down, total, before=None):
    hidden = down.shape[0]
    part = 256 if hidden % 256 == 0 else 128
    for k in range(0, hidden, part):
        u = jnp.dot(x[...], up[:, k : k + part], preferred_element_type=jnp.float32)
        h = twice_gelu(u + b_up[:, k : k + part]).astype(jnp.bfloat16)
        y = jnp.dot(h, down[k : k + part, :], preferred_element_type=jnp.float32)
        if k:
            total[...] += y
        else:
            total[...] = y if before is None else before[...] + y


def rest_kernel(b, layout, chosen, whole, *refs):
    place = layout.place(b)
    refs = list(refs)
    far = refs.pop(0) if chosen[0] < layout.reach - layout.extra(b - 1) else None
    before, gain, shift, *refs = refs
    if far is None:
        conv = before
    else:
        taps, *refs, conv, wide = refs
        add_far(b, layout, place, chosen, far, before, taps, conv, wide)
    if whole:
        up, b_up, down, normed, total = refs
        normalise(b, conv, gain, shift, normed)
        project(normed, up.at[b], b_up.at[b : b + 1], down.at[b], total)
    else:
        normalise(b, conv, gain, shift, refs[0])


def pieces_of(kind, channels, parts):
    if kind == "plain":
        return [(parts[n], parts[n + 1][...], parts[n + 2]) for n in range(0, len(parts), 3)]
    pieces = []
    if kind == "joined":
        for part in parts:
            last = part.shape[0] - MARGIN
            terms = part[last:, :].astype(jnp.float32)
            pieces.append((part.at[:channels], terms[0:1] + terms[1:2], part.at[channels:last]))
        return pieces
    for part, down in zip(parts[::2], parts[1::2]):
        terms = part[channels:, :].astype(jnp.float32)
        pieces.append((part.at[:channels], terms[0:1] + terms[1:2], down))
    return pieces


def add_kernel(kind, channels, x, before, *refs):
    for piece in pieces_of(kind, channels, refs[:-1]):
        project(x, *piece, refs[-1], before)
        before = refs[-1]


def more_kernel(b, layout, chosen, kind, number, begun, x, *refs):
    place = layout.place(b)
    channels, final = layout.channels, b == layout.blocks - 1
    refs = list(refs)
    take = lambda count: [refs.pop(0) for _ in range(count)]
    pieces, first = [], None
    if begun:
        first = refs.pop(0)
    else:
        up, b_up, down = take(3)
        pieces.append((up.at[b], b_up.at[b : b + 1], down.at[b]))
    parts = take(number)
    state, b_down, scale = take(3)
    far_state = None if final else refs.pop(0)
    out = refs.pop(0)
    sends = [] if final else take(2)
    total = refs.pop(0)
    pieces += pieces_of(kind, channels, parts)
    for piece in pieces:
        project(x, *piece, total, first)
        first = total
    count, width, _ = out.shape
    rows, reach = layout.rows, layout.reach
    for n, d in enumerate(chosen):
        if d < 0:
            s = far_state[far_row(layout, b, place, -1 - d), :, :].astype(jnp.float32)
        else:
            at = pl.ds(pl.multiple_of(place[0], MARGIN), width)
            s = state[own_row(layout, b, place, d), at, :].astype(jnp.float32)
        y = 0.5 * first[n * width : (n + 1) * width, :] + b_down[b : b + 1]
        s = s + scale[b : b + 1] * y
        if final:
            out[jnp.where(place[2] == 1, count - 1 - n, n)] = s.astype(out.dtype)
            continue
        if d < 0:
            s = jnp.where(place[4], s, 0.0)
        out[n] = s.astype(out.dtype)
        total[n * width : (n + 1) * width, :] = s
        far, near = sends
        size = near.shape[1]
        s = total[pl.ds(pl.multiple_of(n * width + place[5], 8), size), :].astype(out.dtype)
        if d in layout.far_rows(b + 1):
            far[d - layout.far_rows(b + 1)[0]] = s
        if d >= rows - reach:
            near[d - (rows - reach)] = s


def take(b, place, weights, parts, up, down):
    w_up, _, w_down = weights
    hidden = w_up.shape[2] // parts
    at = place[2] * (w_up.shape[2] // 2) + (place[3] * hidden if parts == 4 else 0)
    at = pl.ds(pl.multiple_of(at, hidden), hidden)
    return at, [(w_up.at[b, :, at], up), (w_down.at[b, at, :], down)]


def in_two_terms(value, terms):
    high = value.astype(jnp.bfloat16).astype(jnp.float32)
    low = (value - high).astype(jnp.bfloat16).astype(jnp.float32)
    row = lax.broadcasted_iota(jnp.int32, terms.shape, 0)
    terms[...] = jnp.where(row == 0, high, jnp.where(row == 1, low, 0.0)).astype(terms.dtype)


def start(copies, sems):
    copies = [pltpu.make_async_copy(*copy, sems.at[n]) for n, copy in enumerate(copies)]
    for copy in copies:
        copy.start()
    return copies


def prepare_kernel(layout, features, *refs):
    place = layout.place(0)
    weights, refs = refs[: 3 if len(refs) > 5 else 0], refs[3 if len(refs) > 5 else 0 :]
    *refs, sems = refs
    if weights:
        *refs, bias, terms = refs
    outs, stages = list(refs[: len(refs) // 2]), list(refs[len(refs) // 2 :])
    at = pl.ds(pl.multiple_of(place[6], MARGIN), outs[0].shape[1])
    sources = []
    for side, out in zip((place[2], 1 - place[2]), outs):
        count = out.shape[0]
        sources.append(features.at[pl.ds(side * (layout.rows - count), count), at])
    if weights:
        channels = layout.channels
        hidden, taken = take(0, place, weights, 4, stages[2].at[:channels], stages[3])
        first = start([*taken, (weights[1], bias)], sems.at[0])
        rest = start(list(zip(sources, stages)), sems.at[1])
        first[2].wait()
        in_two_terms(bias[0:1, hidden], terms)
        first[0].wait()
        legs = [(stages[2].at[:channels], outs[2].at[:channels]), (terms, outs[2].at[channels:])]
        legs = start(legs, sems.at[2])
        first[1].wait()
        legs += start([(stages[3], outs[3])], sems.at[3])
    else:
        rest = start(list(zip(sources, stages)), sems.at[1])
        legs = []
    for n, copy in enumerate(rest):
        copy.wait()
        legs += start([(stages[n], outs[n])], sems.at[4 + n])
    for copy in legs:
        copy.wait()


def pack_kernel(b, layout, w_up, b_up, w_down, out, terms, sems):
    channels, last = layout.channels, out.shape[0] - MARGIN
    outs = out.at[:channels], out.at[channels:last]
    hidden, copies = take(b, layout.place(b), (w_up, b_up, w_down), 2, *outs)
    copies = start(copies, sems.at[0])
    in_two_terms(b_up[b : b + 1, hidden], terms)
    copies += start([(terms, out.at[last:])], sems.at[1])
    for copy in copies:
        copy.wait()


def cost(flops):
    return pl.CostEstimate(flops=flops, bytes_accessed=0, transcendentals=0)


def prepare(layout, features, weights=()):
    _, size = layout.size(*layout.edge(0))
    channels = layout.channels
    shapes = [(count, size, channels) for count in (len(layout.far_rows(0)), layout.reach)]
    scratch = [pltpu.SemaphoreType.DMA((6, 3))]
    if weights:
        hidden = weights[0].shape[2] // 4
        shapes += [(channels + MARGIN, hidden), (hidden, channels)]
        scratch.insert(0, pltpu.VMEM((MARGIN, hidden), jnp.bfloat16))
        scratch.insert(0, pltpu.VMEM(weights[1].shape, jnp.float32))
    return pl.pallas_call(
        functools.partial(prepare_kernel, layout),
        out_shape=[jax.ShapeDtypeStruct(shape, jnp.bfloat16) for shape in shapes],
        in_specs=[HBM] + [HBM] * len(weights),
        out_specs=[HBM] * len(shapes),
        scratch_shapes=[pltpu.VMEM(shape, jnp.bfloat16) for shape in shapes] + scratch,
        compiler_params=COPIES,
        cost_estimate=cost(1),
        name="prepare",
    )(features, *weights)


def pack(b, layout, weights):
    _, channels, hidden = weights[0].shape
    hidden //= 2
    shape = (channels + hidden + MARGIN, channels)
    return pl.pallas_call(
        functools.partial(pack_kernel, b, layout),
        out_shape=jax.ShapeDtypeStruct(shape, jnp.bfloat16),
        in_specs=[HBM, VMEM, HBM],
        out_specs=VMEM,
        scratch_shapes=[
            pltpu.VMEM((MARGIN, hidden), jnp.bfloat16),
            pltpu.SemaphoreType.DMA((2, 2)),
        ],
        compiler_params=PARAMS,
        cost_estimate=cost(1),
        name="pack",
    )(*weights)


def conv_own(b, layout, own, near, taps, bias):
    groups = layout.channels // LANES
    _, width = layout.size(*layout.window(b))
    final = b == layout.blocks - 1
    complete = range(layout.reach - layout.extra(b - 1), layout.rows) if final else range(0)
    counts = [len(layout.result_rows(b)) - len(complete)] + [len(complete)] * final
    lines = len(layout.own_rows(b)) + layout.reach
    return pl.pallas_call(
        functools.partial(own_kernel, b, layout, complete),
        out_shape=[jax.ShapeDtypeStruct((groups, n, width, LANES), jnp.float32) for n in counts],
        in_specs=[VMEM] * 4,
        out_specs=[VMEM] * len(counts),
        scratch_shapes=[pltpu.VMEM((groups, lines, width + 2 * MARGIN, LANES), jnp.float32)],
        compiler_params=PARAMS,
        cost_estimate=cost(1 if final else LONG),
        name="conv_own",
    )(own, near, taps, bias)


def conv_rest(b, layout, chosen, far, before, taps, gain, shift, weights=()):
    groups, rows, width, _ = before.shape
    channels = layout.channels
    args = [before, gain, shift]
    shapes = [jax.ShapeDtypeStruct((rows * width, channels), jnp.bfloat16)]
    scratch = []
    if far is not None:
        args = [far, *args, taps]
        lines = len(layout.far_rows(b))
        scratch.append(pltpu.VMEM((groups, rows, width, LANES), jnp.float32))
        scratch.append(pltpu.VMEM((groups, lines, width + 2 * MARGIN, LANES), jnp.float32))
    if weights:
        args += weights
        shapes.append(jax.ShapeDtypeStruct((rows * width, channels), jnp.float32))
    return pl.pallas_call(
        functools.partial(rest_kernel, b, layout, chosen, bool(weights)),
        out_shape=shapes,
        in_specs=[VMEM] * len(args),
        out_specs=[VMEM] * len(shapes),
        scratch_shapes=scratch,
        compiler_params=PARAMS,
        cost_estimate=cost(1 if weights else LONG),
        name="conv_rest",
    )(*args)


def add(x, before, kind, parts):
    return pl.pallas_call(
        functools.partial(add_kernel, kind, x.shape[1]),
        out_shape=jax.ShapeDtypeStruct(before.shape, jnp.float32),
        in_specs=[VMEM] * (2 + len(parts)),
        out_specs=VMEM,
        compiler_params=PARAMS,
        cost_estimate=cost(1),
        name="add",
    )(x, before, *parts)


def more(b, layout, chosen, x, begun, kind, parts, state, b_down, scale, far=None):
    positions, channels = x.shape
    args = [x, *begun, *parts, state, b_down, scale]
    shapes = [(len(chosen), positions // len(chosen), channels)]
    if far is not None:
        args.append(far)
        _, size = layout.size(*layout.edge(b + 1))
        shapes += [(n, size, channels) for n in (len(layout.far_rows(b + 1)), layout.reach)]
    return pl.pallas_call(
        functools.partial(more_kernel, b, layout, chosen, kind, len(parts), len(begun) == 1),
        out_shape=[jax.ShapeDtypeStruct(shape, jnp.bfloat16) for shape in shapes],
        in_specs=[VMEM] * len(args),
        out_specs=[VMEM] * len(shapes),
        scratch_shapes=[pltpu.VMEM((positions, channels), jnp.float32)],
        compiler_params=PARAMS,
        cost_estimate=cost(1),
        name="more",
    )(*args)


def within(array):
    return lax.ppermute(array, "row", [(i, i ^ 1) for i in range(lax.axis_size("row"))])


def across(array):
    pairs = [(i, i + 1) for i in range(1, lax.axis_size("row") - 1, 2)]
    return lax.ppermute(array, "row", pairs + [(target, source) for source, target in pairs])


def swap_hid(array):
    return lax.ppermute(array, "hid", [(0, 1), (1, 0)])


def swap_row(array, bit):
    return lax.ppermute(array, "row", [(i, i ^ bit) for i in range(lax.axis_size("row"))])


def after(array, *earlier):
    return lax.optimization_barrier((array, *earlier))[0]


def gather(w_up, b_up, w_down):
    number, me = lax.axis_size("hid"), lax.axis_index("hid")
    arrays = [lax.all_gather(a, "hid") for a in (w_up, b_up.reshape(1, -1), w_down)]
    pick = lambda a, k: lax.dynamic_index_in_dim(a, lax.rem(me + k, number), 0, keepdims=False)
    return [pick(a, k) for k in range(1, number) for a in arrays]


def shards(features, dw_weight, dw_bias, ln_gain, ln_bias, w_up, b_up, w_down, b_down, layer_scale):
    layout = Layout(features, dw_weight)
    blocks, rows, number = layout.blocks, layout.rows, layout.number
    me, row, count = lax.axis_index("hid"), lax.axis_index("row"), lax.axis_size("row")
    odd = lax.rem(row, 2)
    pairs = number == 2 and w_up.shape[2] == 2 * layout.channels and count % 8 == 0
    weights = (w_up, b_up, w_down)
    norm, ending = (ln_gain, ln_bias), (b_down, layer_scale)

    outer, inner, *packed = prepare(layout, features, weights if pairs else ())
    far, near = across(outer), within(inner)
    state = features
    if pairs:
        up, down = swap_hid(packed[0]), swap_hid(packed[1])
    for b in range(blocks):
        before, *complete = conv_own(b, layout, state, near, dw_weight, dw_bias)
        if not pairs:
            kind, parts = "plain", gather(w_up[b], b_up[b], w_down[b])
        if b < blocks - 1:
            if pairs:
                later = swap_hid(pack(b + 1, layout, weights))
            if pairs and b == 0:
                down = after(down, before)
                up_other, down_other = swap_row(up, 4), swap_row(down, 4)
            chosen = layout.result_rows(b)
            x, total = conv_rest(b, layout, chosen, far, before, dw_weight, *norm, weights)
            if pairs and b == 0:
                up_other, down_other = after(up_other, total), after(down_other, total)
                mine = [up, down, up_other, down_other]
                kind, parts = "pairs", [within(a) for a in mine]
                total = add(x, total, kind, mine)
            elif pairs:
                kind, parts = "joined", [joined, within(joined)]
            state, outer, inner = more(
                b, layout, chosen, x, (total,), kind, parts, state, *ending, far
            )
            far, near = across(outer), within(inner)
            if pairs:
                joined = later
            continue
        first, last = tuple(range(before.shape[1])), tuple(range(before.shape[1], rows))
        if pairs and b == 0:
            kind, parts = "plain", gather(w_up[b], b_up[b], w_down[b])
        elif pairs:
            joined = after(joined, before)
            kind, parts = "joined", [joined, within(joined)]
        x, total = conv_rest(b, layout, last, None, complete[0], dw_weight, *norm, weights)
        before = after(before, total)
        x_first, = conv_rest(b, layout, first, far, before, dw_weight, *norm)
        total = after(total, x_first)
        inner, = more(b, layout, last, x, (total,), kind, parts, state, *ending)
        outer, = more(b, layout, first, x_first, weights, kind, parts, state, *ending)
    if number == 2:
        def columns_of(a):
            other = swap_hid(a)
            left, right = jnp.where(me == 0, a, other), jnp.where(me == 0, other, a)
            return jnp.concatenate([left, right], axis=1)
    elif number == 1:
        columns_of = lambda a: a
    else:
        columns_of = lambda a: lax.all_gather(a, "hid", axis=1, tiled=True)
    inner, outer = columns_of(inner), columns_of(outer)
    if inner.shape == outer.shape:
        return jnp.concatenate([jnp.where(odd == 1, inner, outer), jnp.where(odd == 1, outer, inner)])
    return jnp.where(odd == 1, jnp.concatenate([inner, outer]), jnp.concatenate([outer, inner]))


def solution(mesh):
    return jax.shard_map(
        shards,
        mesh=mesh,
        in_specs=(
            P("row", None, None),
            P(),
            P(),
            P(),
            P(),
            P(None, None, "hid"),
            P(None, "hid"),
            P(None, "hid", None),
            P(),
            P(),
        ),
        out_specs=P("row", None, None),
        check_vma=False,
    )
```

```python
import functools

import jax
import jax.numpy as jnp
from jax import lax
from jax.experimental import pallas as pl
from jax.experimental.pallas import tpu as pltpu
from jax.sharding import PartitionSpec as P

LANES = 128
MARGIN = 16
LONG = 10**11
ERF = (
    0.7978275766866006,
    0.036469930744144466,
    -0.00012547620415072412,
    -3.0467196783772113e-05,
    1.1126315774795922e-06,
)
VMEM = pl.BlockSpec(memory_space=pltpu.VMEM)
HBM = pl.BlockSpec(memory_space=pltpu.HBM)
PARAMS = pltpu.CompilerParams(vmem_limit_bytes=20 * 1024 * 1024)
COPIES = pltpu.CompilerParams(vmem_limit_bytes=61 * 1024 * 1024)


def twice_gelu(u):
    v = u * u
    p = jnp.full_like(u, ERF[-1])
    for c in ERF[-2::-1]:
        p = p * v + c
    return u + u * jnp.tanh(u * p)


def tile_of(width):
    return next(s for s in (48, 32, 16) if width % s == 0)


class Layout:
    def __init__(self, features, kernels):
        self.blocks, self.reach = kernels.shape[0], kernels.shape[1] // 2
        self.rows, self.columns, self.channels = features.shape
        self.number = lax.axis_size("hid")
        self.width = self.columns // self.number

    def size(self, reach, unit):
        extra = -(-reach // unit) * unit
        return extra, min(self.columns, self.width + (1 if self.number == 2 else 2) * extra)

    def start(self, reach, unit):
        extra, size = self.size(reach, unit)
        return jnp.clip(lax.axis_index("hid") * self.width - extra, 0, self.columns - size)

    def window(self, b):
        return self.reach * (self.blocks - 1 - b), MARGIN

    def edge(self, b):
        return self.reach * (self.blocks - b), 8 if b else MARGIN

    def extra(self, b):
        same = self.size(*self.window(0)) == self.size(*self.edge(0))
        return int(b == 0 and self.blocks > 1 and self.rows > self.reach and same)

    def own_rows(self, b):
        return range(-self.extra(b - 1), self.rows)

    def result_rows(self, b):
        return range(-self.extra(b), self.rows)

    def far_rows(self, b):
        return range(self.extra(b - 1), self.reach + self.extra(b))

    def place(self, b):
        to, halo = self.start(*self.window(b)), self.start(*self.edge(b))
        start = self.start(*self.window(b - 1)) if b else 0
        later = self.start(*self.edge(b + 1))
        row = lax.axis_index("row")
        odd, parity = lax.rem(row, 2), lax.rem(lax.div(row, 4), 2)
        there = jnp.where(odd == 1, row < lax.axis_size("row") - 1, row > 0)
        return to - start, halo - to + MARGIN, odd, parity, there, later - to, halo


def own_row(layout, b, place, d):
    return d + layout.extra(b - 1) if b else jnp.where(place[2] == 1, layout.rows - 1 - d, d)


def far_row(layout, b, place, k):
    rows = layout.far_rows(b)
    return k - rows[0] if b else jnp.where(place[2] == 1, k, len(rows) - 1 - k)


def tap_of(place, t, size):
    return jnp.where(place[2] == 1, size - 1 - t, t)


def convolve(b, place, sums, wide, inputs, outputs, taps, c, lanes, start, step):
    size = taps.shape[1]
    reach = size // 2
    for i, position in enumerate(inputs):
        used = [(n, position - d + reach) for n, d in enumerate(outputs)]
        used = [(n, tap_of(place, t, size)) for n, t in used if 0 <= t < size]
        if not used:
            continue
        for j in range(size):
            first = start + MARGIN + j - reach
            x = wide[c, i, first : first + step]
            for n, t in used:
                sums[n] = sums[n] + x * taps[b, t, j : j + 1, lanes]
    return sums


def own_kernel(b, layout, complete, own, near, taps, bias, *refs):
    place = layout.place(b)
    out, *conv, wide = refs
    groups, _, width, _ = out.shape
    reach = near.shape[0]
    rows, outputs = layout.own_rows(b), layout.result_rows(b)
    fill_own(layout, b, place, own, wide)
    back = place[2] if b == 0 else 1
    sources = [(near, jnp.where(back == 1, reach - 1 - k, k)) for k in range(reach)]
    fill_halo(place, sources, wide, len(rows))
    step = tile_of(width)
    inputs = range(rows[0], layout.rows + reach)

    def group(c, _):
        lanes = pl.ds(pl.multiple_of(c * LANES, LANES), LANES)
        for start in range(0, width, step):
            sums = [jnp.broadcast_to(bias[b : b + 1, lanes], (step, LANES)) for _ in outputs]
            sums = convolve(b, place, sums, wide, inputs, outputs, taps, c, lanes, start, step)
            for n, d in enumerate(outputs):
                if d in complete:
                    conv[0][c, d - complete[0], start : start + step] = sums[n]
                else:
                    out[c, n, start : start + step] = sums[n]
        return 0

    lax.fori_loop(0, groups, group, 0)


def fill_own(layout, b, place, own, wide):
    groups, _, columns, _ = wide.shape
    for k in range(columns // MARGIN):
        at = place[0] + (k - 1) * MARGIN
        inside = (at >= 0) & (at <= own.shape[1] - MARGIN)
        at = pl.multiple_of(jnp.clip(at, 0, own.shape[1] - MARGIN), MARGIN)
        for n, d in enumerate(layout.own_rows(b)):
            for c in range(groups):
                x = own[own_row(layout, b, place, d), pl.ds(at, MARGIN), c * LANES : (c + 1) * LANES]
                x = jnp.where(inside, x.astype(jnp.float32), 0.0)
                wide[c, n, k * MARGIN : (k + 1) * MARGIN] = x


def fill_halo(place, sources, wide, first):
    groups, _, columns, _ = wide.shape
    size = sources[0][0].shape[1]
    at = pl.ds(pl.multiple_of(place[1], 8), size)
    for i, (ref, row) in enumerate(sources):
        for c in range(groups):
            zeros = jnp.zeros((2 * MARGIN, LANES), jnp.float32)
            wide[c, first + i, : 2 * MARGIN] = zeros
            wide[c, first + i, columns - 2 * MARGIN :] = zeros
            x = ref[row, :, c * LANES : (c + 1) * LANES].astype(jnp.float32)
            wide[c, first + i, at] = x


def add_far(b, layout, place, chosen, far, before, taps, conv, wide):
    groups, _, width, _ = before.shape
    rows = layout.far_rows(b)
    fill_halo(place, [(far, far_row(layout, b, place, k)) for k in rows], wide, 0)
    step = tile_of(width)
    inputs = [-1 - k for k in rows]

    def group(c, _):
        lanes = pl.ds(pl.multiple_of(c * LANES, LANES), LANES)
        for start in range(0, width, step):
            sums = [before[c, n, start : start + step] for n in range(len(chosen))]
            sums = convolve(b, place, sums, wide, inputs, chosen, taps, c, lanes, start, step)
            for n in range(len(chosen)):
                conv[c, n, start : start + step] = sums[n]
        return 0

    lax.fori_loop(0, groups, group, 0)


def normalise(b, conv, gain, shift, out):
    groups, rows, width, _ = conv.shape
    channels = groups * LANES
    for r in range(rows):
        x = [conv[c, r].astype(jnp.bfloat16).astype(jnp.float32) for c in range(groups)]
        mean = jnp.sum(functools.reduce(jnp.add, x), axis=1, keepdims=True) * (1.0 / channels)
        x = [v - mean for v in x]
        var = jnp.sum(functools.reduce(jnp.add, [v * v for v in x]), axis=1, keepdims=True)
        scale = lax.rsqrt(var * (1.0 / channels) + 1e-06)
        for c in range(groups):
            lanes = slice(c * LANES, (c + 1) * LANES)
            y = x[c] * scale * gain[b : b + 1, lanes] + shift[b : b + 1, lanes]
            out[r * width : (r + 1) * width, lanes] = y.astype(out.dtype)


def project(x, up, b_up, down, total, before=None):
    hidden = down.shape[0]
    part = 256 if hidden % 256 == 0 else 128
    for k in range(0, hidden, part):
        u = jnp.dot(x[...], up[:, k : k + part], preferred_element_type=jnp.float32)
        h = twice_gelu(u + b_up[:, k : k + part]).astype(jnp.bfloat16)
        y = jnp.dot(h, down[k : k + part, :], preferred_element_type=jnp.float32)
        if k:
            total[...] += y
        else:
            total[...] = y if before is None else before[...] + y


def rest_kernel(b, layout, chosen, whole, *refs):
    place = layout.place(b)
    refs = list(refs)
    far = refs.pop(0) if chosen[0] < layout.reach - layout.extra(b - 1) else None
    before, gain, shift, *refs = refs
    if far is None:
        conv = before
    else:
        taps, *refs, conv, wide = refs
        add_far(b, layout, place, chosen, far, before, taps, conv, wide)
    if whole:
        up, b_up, down, normed, total = refs
        normalise(b, conv, gain, shift, normed)
        project(normed, up.at[b], b_up.at[b : b + 1], down.at[b], total)
    else:
        normalise(b, conv, gain, shift, refs[0])


def pieces_of(kind, channels, parts):
    if kind == "plain":
        return [(parts[n], parts[n + 1][...], parts[n + 2]) for n in range(0, len(parts), 3)]
    pieces = []
    if kind == "joined":
        for part in parts:
            last = part.shape[0] - MARGIN
            terms = part[last:, :].astype(jnp.float32)
            pieces.append((part.at[:channels], terms[0:1] + terms[1:2], part.at[channels:last]))
        return pieces
    for part, down in zip(parts[::2], parts[1::2]):
        terms = part[channels:, :].astype(jnp.float32)
        pieces.append((part.at[:channels], terms[0:1] + terms[1:2], down))
    return pieces


def add_kernel(kind, channels, x, before, *refs):
    for piece in pieces_of(kind, channels, refs[:-1]):
        project(x, *piece, refs[-1], before)
        before = refs[-1]


def more_kernel(b, layout, chosen, kind, number, begun, x, *refs):
    place = layout.place(b)
    channels, final = layout.channels, b == layout.blocks - 1
    refs = list(refs)
    take = lambda count: [refs.pop(0) for _ in range(count)]
    pieces, first = [], None
    if begun:
        first = refs.pop(0)
    else:
        up, b_up, down = take(3)
        pieces.append((up.at[b], b_up.at[b : b + 1], down.at[b]))
    parts = take(number)
    state, b_down, scale = take(3)
    far_state = None if final else refs.pop(0)
    out = refs.pop(0)
    sends = [] if final else take(2)
    total = refs.pop(0)
    pieces += pieces_of(kind, channels, parts)
    for piece in pieces:
        project(x, *piece, total, first)
        first = total
    count, width, _ = out.shape
    rows, reach = layout.rows, layout.reach
    for n, d in enumerate(chosen):
        if d < 0:
            s = far_state[far_row(layout, b, place, -1 - d), :, :].astype(jnp.float32)
        else:
            at = pl.ds(pl.multiple_of(place[0], MARGIN), width)
            s = state[own_row(layout, b, place, d), at, :].astype(jnp.float32)
        y = 0.5 * first[n * width : (n + 1) * width, :] + b_down[b : b + 1]
        s = s + scale[b : b + 1] * y
        if final:
            out[jnp.where(place[2] == 1, count - 1 - n, n)] = s.astype(out.dtype)
            continue
        if d < 0:
            s = jnp.where(place[4], s, 0.0)
        out[n] = s.astype(out.dtype)
        total[n * width : (n + 1) * width, :] = s
        far, near = sends
        size = near.shape[1]
        s = total[pl.ds(pl.multiple_of(n * width + place[5], 8), size), :].astype(out.dtype)
        if d in layout.far_rows(b + 1):
            far[d - layout.far_rows(b + 1)[0]] = s
        if d >= rows - reach:
            near[d - (rows - reach)] = s


def take(b, place, weights, parts, up, down):
    w_up, _, w_down = weights
    hidden = w_up.shape[2] // parts
    at = place[2] * (w_up.shape[2] // 2) + (place[3] * hidden if parts == 4 else 0)
    at = pl.ds(pl.multiple_of(at, hidden), hidden)
    return at, [(w_up.at[b, :, at], up), (w_down.at[b, at, :], down)]


def in_two_terms(value, terms):
    high = value.astype(jnp.bfloat16).astype(jnp.float32)
    low = (value - high).astype(jnp.bfloat16).astype(jnp.float32)
    row = lax.broadcasted_iota(jnp.int32, terms.shape, 0)
    terms[...] = jnp.where(row == 0, high, jnp.where(row == 1, low, 0.0)).astype(terms.dtype)


def start(copies, sems):
    copies = [pltpu.make_async_copy(*copy, sems.at[n]) for n, copy in enumerate(copies)]
    for copy in copies:
        copy.start()
    return copies


def prepare_kernel(layout, features, *refs):
    place = layout.place(0)
    weights, refs = refs[: 3 if len(refs) > 5 else 0], refs[3 if len(refs) > 5 else 0 :]
    *refs, sems = refs
    if weights:
        *refs, bias, terms = refs
    outs, stages = list(refs[: len(refs) // 2]), list(refs[len(refs) // 2 :])
    at = pl.ds(pl.multiple_of(place[6], MARGIN), outs[0].shape[1])
    sources = []
    for side, out in zip((place[2], 1 - place[2]), outs):
        count = out.shape[0]
        sources.append(features.at[pl.ds(side * (layout.rows - count), count), at])
    if outs[0].shape[0] == layout.rows:
        sources.pop()
    if weights:
        channels = layout.channels
        hidden, taken = take(0, place, weights, 4, stages[2].at[:channels], stages[3])
        first = start([*taken, (weights[1], bias)], sems.at[0])
        rest = start(list(zip(sources, stages)), sems.at[1])
        first[2].wait()
        in_two_terms(bias[0:1, hidden], terms)
        first[0].wait()
        legs = [(stages[2].at[:channels], outs[2].at[:channels]), (terms, outs[2].at[channels:])]
        legs = start(legs, sems.at[2])
        first[1].wait()
        legs += start([(stages[3], outs[3])], sems.at[3])
    else:
        rest = start(list(zip(sources, stages)), sems.at[1])
        legs = []
    rest[0].wait()
    if outs[0].shape[0] == layout.rows:
        inner = stages[0].at[pl.ds((1 - place[2]) * (layout.rows - layout.reach), layout.reach)]
    else:
        rest[1].wait()
        inner = stages[1]
    legs += start([(stages[0], outs[0]), (inner, outs[1])], sems.at[4])
    for copy in legs:
        copy.wait()


def pack_kernel(b, layout, w_up, b_up, w_down, out, terms, sems):
    channels, last = layout.channels, out.shape[0] - MARGIN
    outs = out.at[:channels], out.at[channels:last]
    hidden, copies = take(b, layout.place(b), (w_up, b_up, w_down), 2, *outs)
    copies = start(copies, sems.at[0])
    in_two_terms(b_up[b : b + 1, hidden], terms)
    copies += start([(terms, out.at[last:])], sems.at[1])
    for copy in copies:
        copy.wait()


def cost(flops):
    return pl.CostEstimate(flops=flops, bytes_accessed=0, transcendentals=0)


def prepare(layout, features, weights=()):
    _, size = layout.size(*layout.edge(0))
    channels = layout.channels
    shapes = [(count, size, channels) for count in (len(layout.far_rows(0)), layout.reach)]
    scratch = [pltpu.SemaphoreType.DMA((6, 3))]
    if weights:
        hidden = weights[0].shape[2] // 4
        shapes += [(channels + MARGIN, hidden), (hidden, channels)]
        scratch.insert(0, pltpu.VMEM((MARGIN, hidden), jnp.bfloat16))
        scratch.insert(0, pltpu.VMEM(weights[1].shape, jnp.float32))
    return pl.pallas_call(
        functools.partial(prepare_kernel, layout),
        out_shape=[jax.ShapeDtypeStruct(shape, jnp.bfloat16) for shape in shapes],
        in_specs=[HBM] + [HBM] * len(weights),
        out_specs=[HBM] * len(shapes),
        scratch_shapes=[pltpu.VMEM(shape, jnp.bfloat16) for shape in shapes] + scratch,
        compiler_params=COPIES,
        cost_estimate=cost(1),
        name="prepare",
    )(features, *weights)


def pack(b, layout, weights):
    _, channels, hidden = weights[0].shape
    hidden //= 2
    shape = (channels + hidden + MARGIN, channels)
    return pl.pallas_call(
        functools.partial(pack_kernel, b, layout),
        out_shape=jax.ShapeDtypeStruct(shape, jnp.bfloat16),
        in_specs=[HBM, VMEM, HBM],
        out_specs=VMEM,
        scratch_shapes=[
            pltpu.VMEM((MARGIN, hidden), jnp.bfloat16),
            pltpu.SemaphoreType.DMA((2, 2)),
        ],
        compiler_params=PARAMS,
        cost_estimate=cost(1),
        name="pack",
    )(*weights)


def conv_own(b, layout, own, near, taps, bias):
    groups = layout.channels // LANES
    _, width = layout.size(*layout.window(b))
    final = b == layout.blocks - 1
    complete = range(layout.reach - layout.extra(b - 1), layout.rows) if final else range(0)
    counts = [len(layout.result_rows(b)) - len(complete)] + [len(complete)] * final
    lines = len(layout.own_rows(b)) + layout.reach
    return pl.pallas_call(
        functools.partial(own_kernel, b, layout, complete),
        out_shape=[jax.ShapeDtypeStruct((groups, n, width, LANES), jnp.float32) for n in counts],
        in_specs=[VMEM] * 4,
        out_specs=[VMEM] * len(counts),
        scratch_shapes=[pltpu.VMEM((groups, lines, width + 2 * MARGIN, LANES), jnp.float32)],
        compiler_params=PARAMS,
        cost_estimate=cost(1 if final else LONG),
        name="conv_own",
    )(own, near, taps, bias)


def conv_rest(b, layout, chosen, far, before, taps, gain, shift, weights=()):
    groups, rows, width, _ = before.shape
    channels = layout.channels
    args = [before, gain, shift]
    shapes = [jax.ShapeDtypeStruct((rows * width, channels), jnp.bfloat16)]
    scratch = []
    if far is not None:
        args = [far, *args, taps]
        lines = len(layout.far_rows(b))
        scratch.append(pltpu.VMEM((groups, rows, width, LANES), jnp.float32))
        scratch.append(pltpu.VMEM((groups, lines, width + 2 * MARGIN, LANES), jnp.float32))
    if weights:
        args += weights
        shapes.append(jax.ShapeDtypeStruct((rows * width, channels), jnp.float32))
    return pl.pallas_call(
        functools.partial(rest_kernel, b, layout, chosen, bool(weights)),
        out_shape=shapes,
        in_specs=[VMEM] * len(args),
        out_specs=[VMEM] * len(shapes),
        scratch_shapes=scratch,
        compiler_params=PARAMS,
        cost_estimate=cost(1 if weights else LONG),
        name="conv_rest",
    )(*args)


def add(x, before, kind, parts):
    return pl.pallas_call(
        functools.partial(add_kernel, kind, x.shape[1]),
        out_shape=jax.ShapeDtypeStruct(before.shape, jnp.float32),
        in_specs=[VMEM] * (2 + len(parts)),
        out_specs=VMEM,
        compiler_params=PARAMS,
        cost_estimate=cost(1),
        name="add",
    )(x, before, *parts)


def more(b, layout, chosen, x, begun, kind, parts, state, b_down, scale, far=None):
    positions, channels = x.shape
    args = [x, *begun, *parts, state, b_down, scale]
    shapes = [(len(chosen), positions // len(chosen), channels)]
    if far is not None:
        args.append(far)
        _, size = layout.size(*layout.edge(b + 1))
        shapes += [(n, size, channels) for n in (len(layout.far_rows(b + 1)), layout.reach)]
    return pl.pallas_call(
        functools.partial(more_kernel, b, layout, chosen, kind, len(parts), len(begun) == 1),
        out_shape=[jax.ShapeDtypeStruct(shape, jnp.bfloat16) for shape in shapes],
        in_specs=[VMEM] * len(args),
        out_specs=[VMEM] * len(shapes),
        scratch_shapes=[pltpu.VMEM((positions, channels), jnp.float32)],
        compiler_params=PARAMS,
        cost_estimate=cost(1),
        name="more",
    )(*args)


def assemble_kernel(layout, kinds, *refs):
    *parts, out, sems = refs
    parts = parts[len(parts) - len(kinds) :]
    _, _, odd, *_ = layout.place(layout.blocks - 1)
    copies = []
    for part, (outer, other) in zip(parts, kinds):
        count = part.shape[0]
        row = jnp.where(odd == outer, layout.rows - count, 0)
        me = lax.axis_index("hid")
        column = pl.multiple_of((1 - me if other else me) * layout.width, MARGIN)
        copies.append((part, out.at[pl.ds(row, count), pl.ds(column, layout.width)]))
    for copy in start(copies, sems):
        copy.wait()


def assemble(layout, out, parts):
    anywhere = pl.BlockSpec(memory_space=pl.ANY)
    shape = (layout.rows, layout.columns, layout.channels)
    args = ([] if out is None else [out]) + [part for part, *_ in parts]
    return pl.pallas_call(
        functools.partial(assemble_kernel, layout, [kind for _, *kind in parts]),
        out_shape=jax.ShapeDtypeStruct(shape, jnp.bfloat16),
        in_specs=([] if out is None else [anywhere]) + [VMEM] * len(parts),
        out_specs=anywhere,
        scratch_shapes=[pltpu.SemaphoreType.DMA((len(parts),))],
        input_output_aliases={} if out is None else {0: 0},
        compiler_params=PARAMS,
        cost_estimate=cost(1),
        name="assemble",
    )(*args)


def within(array):
    return lax.ppermute(array, "row", [(i, i ^ 1) for i in range(lax.axis_size("row"))])


def across(array):
    pairs = [(i, i + 1) for i in range(1, lax.axis_size("row") - 1, 2)]
    return lax.ppermute(array, "row", pairs + [(target, source) for source, target in pairs])


def swap_hid(array):
    return lax.ppermute(array, "hid", [(0, 1), (1, 0)])


def swap_row(array, bit):
    return lax.ppermute(array, "row", [(i, i ^ bit) for i in range(lax.axis_size("row"))])


def after(array, *earlier):
    return lax.optimization_barrier((array, *earlier))[0]


def gather(w_up, b_up, w_down):
    number, me = lax.axis_size("hid"), lax.axis_index("hid")
    arrays = [lax.all_gather(a, "hid") for a in (w_up, b_up.reshape(1, -1), w_down)]
    pick = lambda a, k: lax.dynamic_index_in_dim(a, lax.rem(me + k, number), 0, keepdims=False)
    return [pick(a, k) for k in range(1, number) for a in arrays]


def shards(features, dw_weight, dw_bias, ln_gain, ln_bias, w_up, b_up, w_down, b_down, layer_scale):
    layout = Layout(features, dw_weight)
    blocks, rows, number = layout.blocks, layout.rows, layout.number
    me, row, count = lax.axis_index("hid"), lax.axis_index("row"), lax.axis_size("row")
    odd = lax.rem(row, 2)
    pairs = number == 2 and w_up.shape[2] == 2 * layout.channels and count % 8 == 0
    weights = (w_up, b_up, w_down)
    norm, ending = (ln_gain, ln_bias), (b_down, layer_scale)

    outer, inner, *packed = prepare(layout, features, weights if pairs else ())
    far, near = across(outer), within(inner)
    state = features
    if pairs:
        up, down = swap_hid(packed[0]), swap_hid(packed[1])
    for b in range(blocks):
        before, *complete = conv_own(b, layout, state, near, dw_weight, dw_bias)
        if not pairs:
            kind, parts = "plain", gather(w_up[b], b_up[b], w_down[b])
        if b < blocks - 1:
            if pairs:
                later = swap_hid(pack(b + 1, layout, weights))
            if pairs and b == 0:
                down = after(down, before)
                up_other, down_other = swap_row(up, 4), swap_row(down, 4)
            chosen = layout.result_rows(b)
            x, total = conv_rest(b, layout, chosen, far, before, dw_weight, *norm, weights)
            if pairs and b == 0:
                up_other, down_other = after(up_other, total), after(down_other, total)
                mine = [up, down, up_other, down_other]
                kind, parts = "pairs", [within(a) for a in mine]
                total = add(x, total, kind, mine)
            elif pairs:
                kind, parts = "joined", [joined, within(joined)]
            state, outer, inner = more(
                b, layout, chosen, x, (total,), kind, parts, state, *ending, far
            )
            far, near = across(outer), within(inner)
            if pairs:
                joined = later
            continue
        first, last = tuple(range(before.shape[1])), tuple(range(before.shape[1], rows))
        x, total = conv_rest(b, layout, last, None, complete[0], dw_weight, *norm, weights)
        before, rest = after(before, total), parts if not pairs else None
        if pairs and b == 0:
            kind, parts = "plain", gather(w_up[b], b_up[b], w_down[b])
            rest = parts
        elif pairs:
            joined = after(joined, total)
            kind, rest = "joined", [within(joined)]
            parts = [joined, *rest]
            total = add(x, total, kind, [joined])
        x_first, = conv_rest(b, layout, first, far, before, dw_weight, *norm)
        total = after(total, x_first)
        inner, = more(b, layout, last, x, (total,), kind, rest, state, *ending)
        outer, = more(b, layout, first, x_first, weights, kind, parts, state, *ending)
    if number == 2:
        later = swap_hid(inner), swap_hid(outer)
        out = assemble(layout, None, [(inner, 0, 0), (outer, 1, 0), (later[0], 0, 1)])
        return assemble(layout, out, [(later[1], 1, 1)])
    if number > 2:
        inner, outer = (lax.all_gather(a, "hid", axis=1, tiled=True) for a in (inner, outer))
    if inner.shape == outer.shape:
        return jnp.concatenate([jnp.where(odd == 1, inner, outer), jnp.where(odd == 1, outer, inner)])
    return jnp.where(odd == 1, jnp.concatenate([inner, outer]), jnp.concatenate([outer, inner]))


def solution(mesh):
    return jax.shard_map(
        shards,
        mesh=mesh,
        in_specs=(
            P("row", None, None),
            P(),
            P(),
            P(),
            P(),
            P(None, None, "hid"),
            P(None, "hid"),
            P(None, "hid", None),
            P(),
            P(),
        ),
        out_specs=P("row", None, None),
        check_vma=False,
    )
```

```python
import functools

import jax
import jax.numpy as jnp
from jax import lax
from jax.experimental import pallas as pl
from jax.experimental.pallas import tpu as pltpu
from jax.sharding import PartitionSpec as P

LANES = 128
MARGIN = 16
LONG = 10**11
ERF = (
    0.7978275766866006,
    0.036469930744144466,
    -0.00012547620415072412,
    -3.0467196783772113e-05,
    1.1126315774795922e-06,
)
VMEM = pl.BlockSpec(memory_space=pltpu.VMEM)
HBM = pl.BlockSpec(memory_space=pltpu.HBM)
PARAMS = pltpu.CompilerParams(vmem_limit_bytes=20 * 1024 * 1024)
COPIES = pltpu.CompilerParams(vmem_limit_bytes=61 * 1024 * 1024)


def twice_gelu(u):
    v = u * u
    p = jnp.full_like(u, ERF[-1])
    for c in ERF[-2::-1]:
        p = p * v + c
    return u + u * jnp.tanh(u * p)


def tile_of(width):
    return next(s for s in (48, 32, 16) if width % s == 0)


class Layout:
    def __init__(self, features, kernels):
        self.blocks, self.reach = kernels.shape[0], kernels.shape[1] // 2
        self.rows, self.columns, self.channels = features.shape
        self.number = lax.axis_size("hid")
        self.width = self.columns // self.number

    def size(self, reach, unit):
        extra = -(-reach // unit) * unit
        return extra, min(self.columns, self.width + (1 if self.number == 2 else 2) * extra)

    def start(self, reach, unit):
        extra, size = self.size(reach, unit)
        return jnp.clip(lax.axis_index("hid") * self.width - extra, 0, self.columns - size)

    def window(self, b):
        return self.reach * (self.blocks - 1 - b), MARGIN

    def edge(self, b):
        return self.reach * (self.blocks - b), 8 if b else MARGIN

    def extra(self, b):
        same = self.size(*self.window(0)) == self.size(*self.edge(0))
        return int(b == 0 and self.blocks > 1 and self.rows > self.reach and same)

    def own_rows(self, b):
        return range(-self.extra(b - 1), self.rows)

    def result_rows(self, b):
        return range(-self.extra(b), self.rows)

    def far_rows(self, b):
        return range(self.extra(b - 1), self.reach + self.extra(b))

    def place(self, b):
        to, halo = self.start(*self.window(b)), self.start(*self.edge(b))
        start = self.start(*self.window(b - 1)) if b else 0
        later = self.start(*self.edge(b + 1))
        row = lax.axis_index("row")
        odd, parity = lax.rem(row, 2), lax.rem(lax.div(row, 4), 2)
        there = jnp.where(odd == 1, row < lax.axis_size("row") - 1, row > 0)
        return to - start, halo - to + MARGIN, odd, parity, there, later - to, halo


def own_row(layout, b, place, d):
    return d + layout.extra(b - 1) if b else jnp.where(place[2] == 1, layout.rows - 1 - d, d)


def far_row(layout, b, place, k):
    rows = layout.far_rows(b)
    return k - rows[0] if b else jnp.where(place[2] == 1, k, len(rows) - 1 - k)


def tap_of(place, t, size):
    return jnp.where(place[2] == 1, size - 1 - t, t)


def convolve(b, place, sums, wide, inputs, outputs, taps, c, lanes, start, step):
    size = taps.shape[1]
    reach = size // 2
    for i, position in enumerate(inputs):
        used = [(n, position - d + reach) for n, d in enumerate(outputs)]
        used = [(n, tap_of(place, t, size)) for n, t in used if 0 <= t < size]
        if not used:
            continue
        for j in range(size):
            first = start + MARGIN + j - reach
            x = wide[c, i, first : first + step]
            for n, t in used:
                sums[n] = sums[n] + x * taps[b, t, j : j + 1, lanes]
    return sums


def own_kernel(b, layout, complete, own, near, taps, bias, *refs):
    place = layout.place(b)
    out, *conv, wide = refs
    groups, _, width, _ = out.shape
    reach = near.shape[0]
    rows, outputs = layout.own_rows(b), layout.result_rows(b)
    fill_own(layout, b, place, own, wide)
    back = place[2] if b == 0 else 1
    sources = [(near, jnp.where(back == 1, reach - 1 - k, k)) for k in range(reach)]
    fill_halo(place, sources, wide, len(rows))
    step = tile_of(width)
    inputs = range(rows[0], layout.rows + reach)

    def group(c, _):
        lanes = pl.ds(pl.multiple_of(c * LANES, LANES), LANES)
        for start in range(0, width, step):
            sums = [jnp.broadcast_to(bias[b : b + 1, lanes], (step, LANES)) for _ in outputs]
            sums = convolve(b, place, sums, wide, inputs, outputs, taps, c, lanes, start, step)
            for n, d in enumerate(outputs):
                if d in complete:
                    conv[0][c, d - complete[0], start : start + step] = sums[n]
                else:
                    out[c, n, start : start + step] = sums[n]
        return 0

    lax.fori_loop(0, groups, group, 0)


def fill_own(layout, b, place, own, wide):
    groups, _, columns, _ = wide.shape
    for k in range(columns // MARGIN):
        at = place[0] + (k - 1) * MARGIN
        inside = (at >= 0) & (at <= own.shape[1] - MARGIN)
        at = pl.multiple_of(jnp.clip(at, 0, own.shape[1] - MARGIN), MARGIN)
        for n, d in enumerate(layout.own_rows(b)):
            for c in range(groups):
                x = own[own_row(layout, b, place, d), pl.ds(at, MARGIN), c * LANES : (c + 1) * LANES]
                x = jnp.where(inside, x.astype(jnp.float32), 0.0)
                wide[c, n, k * MARGIN : (k + 1) * MARGIN] = x


def fill_halo(place, sources, wide, first):
    groups, _, columns, _ = wide.shape
    size = sources[0][0].shape[1]
    at = pl.ds(pl.multiple_of(place[1], 8), size)
    for i, (ref, row) in enumerate(sources):
        for c in range(groups):
            zeros = jnp.zeros((2 * MARGIN, LANES), jnp.float32)
            wide[c, first + i, : 2 * MARGIN] = zeros
            wide[c, first + i, columns - 2 * MARGIN :] = zeros
            x = ref[row, :, c * LANES : (c + 1) * LANES].astype(jnp.float32)
            wide[c, first + i, at] = x


def add_far(b, layout, place, chosen, far, before, taps, conv, wide):
    groups, _, width, _ = before.shape
    rows = layout.far_rows(b)
    fill_halo(place, [(far, far_row(layout, b, place, k)) for k in rows], wide, 0)
    step = tile_of(width)
    inputs = [-1 - k for k in rows]

    def group(c, _):
        lanes = pl.ds(pl.multiple_of(c * LANES, LANES), LANES)
        for start in range(0, width, step):
            sums = [before[c, n, start : start + step] for n in range(len(chosen))]
            sums = convolve(b, place, sums, wide, inputs, chosen, taps, c, lanes, start, step)
            for n in range(len(chosen)):
                conv[c, n, start : start + step] = sums[n]
        return 0

    lax.fori_loop(0, groups, group, 0)


def normalise(b, conv, gain, shift, out):
    groups, rows, width, _ = conv.shape
    channels = groups * LANES
    for r in range(rows):
        x = [conv[c, r].astype(jnp.bfloat16).astype(jnp.float32) for c in range(groups)]
        mean = jnp.sum(functools.reduce(jnp.add, x), axis=1, keepdims=True) * (1.0 / channels)
        x = [v - mean for v in x]
        var = jnp.sum(functools.reduce(jnp.add, [v * v for v in x]), axis=1, keepdims=True)
        scale = lax.rsqrt(var * (1.0 / channels) + 1e-06)
        for c in range(groups):
            lanes = slice(c * LANES, (c + 1) * LANES)
            y = x[c] * scale * gain[b : b + 1, lanes] + shift[b : b + 1, lanes]
            out[r * width : (r + 1) * width, lanes] = y.astype(out.dtype)


def project(x, up, b_up, down, total, before=None):
    hidden = down.shape[0]
    part = 256 if hidden % 256 == 0 else 128
    for k in range(0, hidden, part):
        u = jnp.dot(x[...], up[:, k : k + part], preferred_element_type=jnp.float32)
        h = twice_gelu(u + b_up[:, k : k + part]).astype(jnp.bfloat16)
        y = jnp.dot(h, down[k : k + part, :], preferred_element_type=jnp.float32)
        if k:
            total[...] += y
        else:
            total[...] = y if before is None else before[...] + y


def rest_kernel(b, layout, chosen, whole, *refs):
    place = layout.place(b)
    refs = list(refs)
    far = refs.pop(0) if chosen[0] < layout.reach - layout.extra(b - 1) else None
    before, gain, shift, *refs = refs
    if far is None:
        conv = before
    else:
        taps, *refs, conv, wide = refs
        add_far(b, layout, place, chosen, far, before, taps, conv, wide)
    if whole:
        up, b_up, down, normed, total = refs
        normalise(b, conv, gain, shift, normed)
        project(normed, up.at[b], b_up.at[b : b + 1], down.at[b], total)
    else:
        normalise(b, conv, gain, shift, refs[0])


def pieces_of(kind, layout, b, parts):
    channels = layout.channels
    if kind == "plain":
        return [(parts[n], parts[n + 1][...], parts[n + 2]) for n in range(0, len(parts), 3)]

    def bias(part):
        terms = part[channels:, :].astype(jnp.float32)
        return terms[2 * b : 2 * b + 1] + terms[2 * b + 1 : 2 * b + 2]

    if kind == "pairs":
        return [(p.at[:channels], bias(p), q) for p, q in zip(parts[::2], parts[1::2])]
    pieces, parity = [], layout.place(b)[3]
    for part, mine, other in zip(parts[::3], parts[1::3], parts[2::3]):
        mine, other = bias(mine), bias(other)
        halves = jnp.where(parity == 0, mine, other), jnp.where(parity == 0, other, mine)
        half = mine.shape[1]
        for n in range(2):
            columns = slice(n * half, (n + 1) * half)
            down = part.at[channels + n * half : channels + (n + 1) * half]
            pieces.append((part.at[:channels, columns], halves[n], down))
    return pieces


def add_kernel(b, layout, kind, x, before, *refs):
    for piece in pieces_of(kind, layout, b, refs[:-1]):
        project(x, *piece, refs[-1], before)
        before = refs[-1]


def more_kernel(b, layout, chosen, kind, number, begun, x, *refs):
    place = layout.place(b)
    final = b == layout.blocks - 1
    refs = list(refs)
    take = lambda count: [refs.pop(0) for _ in range(count)]
    pieces, first = [], None
    if begun:
        first = refs.pop(0)
    else:
        up, b_up, down = take(3)
        pieces.append((up.at[b], b_up.at[b : b + 1], down.at[b]))
    parts = take(number)
    state, b_down, scale = take(3)
    far_state = None if final else refs.pop(0)
    out = refs.pop(0)
    sends = [] if final else take(2)
    total = refs.pop(0)
    pieces += pieces_of(kind, layout, b, parts)
    for piece in pieces:
        project(x, *piece, total, first)
        first = total
    count, width, _ = out.shape
    rows, reach = layout.rows, layout.reach
    for n, d in enumerate(chosen):
        if d < 0:
            s = far_state[far_row(layout, b, place, -1 - d), :, :].astype(jnp.float32)
        else:
            at = pl.ds(pl.multiple_of(place[0], MARGIN), width)
            s = state[own_row(layout, b, place, d), at, :].astype(jnp.float32)
        y = 0.5 * first[n * width : (n + 1) * width, :] + b_down[b : b + 1]
        s = s + scale[b : b + 1] * y
        if final:
            out[jnp.where(place[2] == 1, count - 1 - n, n)] = s.astype(out.dtype)
            continue
        if d < 0:
            s = jnp.where(place[4], s, 0.0)
        out[n] = s.astype(out.dtype)
        total[n * width : (n + 1) * width, :] = s
        far, near = sends
        size = near.shape[1]
        s = total[pl.ds(pl.multiple_of(n * width + place[5], 8), size), :].astype(out.dtype)
        if d in layout.far_rows(b + 1):
            far[d - layout.far_rows(b + 1)[0]] = s
        if d >= rows - reach:
            near[d - (rows - reach)] = s


def take(b, place, weights, parts, up, down):
    w_up, w_down = weights
    hidden = w_up.shape[2] // parts
    at = place[2] * (w_up.shape[2] // 2) + (place[3] * hidden if parts == 4 else 0)
    at = pl.ds(pl.multiple_of(at, hidden), hidden)
    return at, [(w_up.at[b, :, at], up), (w_down.at[b, at, :], down)]


def in_two_terms(value, terms, first=0):
    high = value.astype(jnp.bfloat16).astype(jnp.float32)
    low = (value - high).astype(jnp.bfloat16).astype(jnp.float32)
    row = lax.broadcasted_iota(jnp.int32, terms.shape, 0)
    rest = terms[...].astype(jnp.float32) if first else 0.0
    both = jnp.where(row == first, high, jnp.where(row == first + 1, low, rest))
    terms[...] = both.astype(terms.dtype)


def start(copies, sems):
    copies = [pltpu.make_async_copy(*copy, sems.at[n]) for n, copy in enumerate(copies)]
    for copy in copies:
        copy.start()
    return copies


def prepare_kernel(layout, features, *refs):
    place = layout.place(0)
    weights, refs = refs[: 3 if len(refs) > 5 else 0], refs[3 if len(refs) > 5 else 0 :]
    *refs, sems = refs
    if weights:
        *refs, bias, terms = refs
    outs, stages = list(refs[: len(refs) // 2]), list(refs[len(refs) // 2 :])
    at = pl.ds(pl.multiple_of(place[6], MARGIN), outs[0].shape[1])
    sources = []
    for side, out in zip((place[2], 1 - place[2]), outs):
        count = out.shape[0]
        sources.append(features.at[pl.ds(side * (layout.rows - count), count), at])
    if outs[0].shape[0] == layout.rows:
        sources.pop()
    if weights:
        channels = layout.channels
        hidden, taken = take(0, place, weights[::2], 4, stages[2].at[:channels], stages[3])
        first = start([*taken, (weights[1], bias)], sems.at[0])
        rest = start(list(zip(sources, stages)), sems.at[1])
        first[2].wait()
        for b in range(layout.blocks):
            in_two_terms(bias[b : b + 1, hidden], terms, 2 * b)
        first[0].wait()
        legs = [(stages[2].at[:channels], outs[2].at[:channels]), (terms, outs[2].at[channels:])]
        legs = start(legs, sems.at[2])
        first[1].wait()
        legs += start([(stages[3], outs[3])], sems.at[3])
    else:
        rest = start(list(zip(sources, stages)), sems.at[1])
        legs = []
    rest[0].wait()
    if outs[0].shape[0] == layout.rows:
        inner = stages[0].at[pl.ds((1 - place[2]) * (layout.rows - layout.reach), layout.reach)]
    else:
        rest[1].wait()
        inner = stages[1]
    legs += start([(stages[0], outs[0]), (inner, outs[1])], sems.at[4])
    for copy in legs:
        copy.wait()


def pack_kernel(b, layout, w_up, w_down, out, sems):
    channels = layout.channels
    copies = take(b, layout.place(b), (w_up, w_down), 2, out.at[:channels], out.at[channels:])[1]
    for copy in start(copies, sems):
        copy.wait()


def cost(flops):
    return pl.CostEstimate(flops=flops, bytes_accessed=0, transcendentals=0)


def prepare(layout, features, weights=()):
    _, size = layout.size(*layout.edge(0))
    channels = layout.channels
    shapes = [(count, size, channels) for count in (len(layout.far_rows(0)), layout.reach)]
    scratch = [pltpu.SemaphoreType.DMA((6, 3))]
    if weights:
        hidden = weights[0].shape[2] // 4
        shapes += [(channels + MARGIN, hidden), (hidden, channels)]
        scratch.insert(0, pltpu.VMEM((MARGIN, hidden), jnp.bfloat16))
        scratch.insert(0, pltpu.VMEM(weights[1].shape, jnp.float32))
    return pl.pallas_call(
        functools.partial(prepare_kernel, layout),
        out_shape=[jax.ShapeDtypeStruct(shape, jnp.bfloat16) for shape in shapes],
        in_specs=[HBM] + [HBM] * len(weights),
        out_specs=[HBM] * len(shapes),
        scratch_shapes=[pltpu.VMEM(shape, jnp.bfloat16) for shape in shapes] + scratch,
        compiler_params=COPIES,
        cost_estimate=cost(1),
        name="prepare",
    )(features, *weights)


def pack(b, layout, weights):
    _, channels, hidden = weights[0].shape
    shape = (channels + hidden // 2, channels)
    return pl.pallas_call(
        functools.partial(pack_kernel, b, layout),
        out_shape=jax.ShapeDtypeStruct(shape, jnp.bfloat16),
        in_specs=[HBM, HBM],
        out_specs=VMEM,
        scratch_shapes=[pltpu.SemaphoreType.DMA((2,))],
        compiler_params=PARAMS,
        cost_estimate=cost(1),
        name="pack",
    )(*weights[::2])


def conv_own(b, layout, own, near, taps, bias):
    groups = layout.channels // LANES
    _, width = layout.size(*layout.window(b))
    final = b == layout.blocks - 1
    complete = range(layout.reach - layout.extra(b - 1), layout.rows) if final else range(0)
    counts = [len(layout.result_rows(b)) - len(complete)] + [len(complete)] * final
    lines = len(layout.own_rows(b)) + layout.reach
    return pl.pallas_call(
        functools.partial(own_kernel, b, layout, complete),
        out_shape=[jax.ShapeDtypeStruct((groups, n, width, LANES), jnp.float32) for n in counts],
        in_specs=[VMEM] * 4,
        out_specs=[VMEM] * len(counts),
        scratch_shapes=[pltpu.VMEM((groups, lines, width + 2 * MARGIN, LANES), jnp.float32)],
        compiler_params=PARAMS,
        cost_estimate=cost(1 if final else LONG),
        name="conv_own",
    )(own, near, taps, bias)


def conv_rest(b, layout, chosen, far, before, taps, gain, shift, weights=()):
    groups, rows, width, _ = before.shape
    channels = layout.channels
    args = [before, gain, shift]
    shapes = [jax.ShapeDtypeStruct((rows * width, channels), jnp.bfloat16)]
    scratch = []
    if far is not None:
        args = [far, *args, taps]
        lines = len(layout.far_rows(b))
        scratch.append(pltpu.VMEM((groups, rows, width, LANES), jnp.float32))
        scratch.append(pltpu.VMEM((groups, lines, width + 2 * MARGIN, LANES), jnp.float32))
    if weights:
        args += weights
        shapes.append(jax.ShapeDtypeStruct((rows * width, channels), jnp.float32))
    return pl.pallas_call(
        functools.partial(rest_kernel, b, layout, chosen, bool(weights)),
        out_shape=shapes,
        in_specs=[VMEM] * len(args),
        out_specs=[VMEM] * len(shapes),
        scratch_shapes=scratch,
        compiler_params=PARAMS,
        cost_estimate=cost(1 if weights else LONG),
        name="conv_rest",
    )(*args)


def add(b, layout, x, before, kind, parts):
    return pl.pallas_call(
        functools.partial(add_kernel, b, layout, kind),
        out_shape=jax.ShapeDtypeStruct(before.shape, jnp.float32),
        in_specs=[VMEM] * (2 + len(parts)),
        out_specs=VMEM,
        compiler_params=PARAMS,
        cost_estimate=cost(1),
        name="add",
    )(x, before, *parts)


def more(b, layout, chosen, x, begun, kind, parts, state, b_down, scale, far=None):
    positions, channels = x.shape
    args = [x, *begun, *parts, state, b_down, scale]
    shapes = [(len(chosen), positions // len(chosen), channels)]
    if far is not None:
        args.append(far)
        _, size = layout.size(*layout.edge(b + 1))
        shapes += [(n, size, channels) for n in (len(layout.far_rows(b + 1)), layout.reach)]
    return pl.pallas_call(
        functools.partial(more_kernel, b, layout, chosen, kind, len(parts), len(begun) == 1),
        out_shape=[jax.ShapeDtypeStruct(shape, jnp.bfloat16) for shape in shapes],
        in_specs=[VMEM] * len(args),
        out_specs=[VMEM] * len(shapes),
        scratch_shapes=[pltpu.VMEM((positions, channels), jnp.float32)],
        compiler_params=PARAMS,
        cost_estimate=cost(1),
        name="more",
    )(*args)


def assemble_kernel(layout, kinds, *refs):
    *parts, out, sems = refs
    parts = parts[len(parts) - len(kinds) :]
    _, _, odd, *_ = layout.place(layout.blocks - 1)
    copies = []
    for part, (outer, other) in zip(parts, kinds):
        count = part.shape[0]
        row = jnp.where(odd == outer, layout.rows - count, 0)
        me = lax.axis_index("hid")
        column = pl.multiple_of((1 - me if other else me) * layout.width, MARGIN)
        copies.append((part, out.at[pl.ds(row, count), pl.ds(column, layout.width)]))
    for copy in start(copies, sems):
        copy.wait()


def assemble(layout, out, parts):
    anywhere = pl.BlockSpec(memory_space=pl.ANY)
    shape = (layout.rows, layout.columns, layout.channels)
    args = ([] if out is None else [out]) + [part for part, *_ in parts]
    return pl.pallas_call(
        functools.partial(assemble_kernel, layout, [kind for _, *kind in parts]),
        out_shape=jax.ShapeDtypeStruct(shape, jnp.bfloat16),
        in_specs=([] if out is None else [anywhere]) + [VMEM] * len(parts),
        out_specs=anywhere,
        scratch_shapes=[pltpu.SemaphoreType.DMA((len(parts),))],
        input_output_aliases={} if out is None else {0: 0},
        compiler_params=PARAMS,
        cost_estimate=cost(1),
        name="assemble",
    )(*args)


def within(array):
    return lax.ppermute(array, "row", [(i, i ^ 1) for i in range(lax.axis_size("row"))])


def across(array):
    pairs = [(i, i + 1) for i in range(1, lax.axis_size("row") - 1, 2)]
    return lax.ppermute(array, "row", pairs + [(target, source) for source, target in pairs])


def swap_hid(array):
    return lax.ppermute(array, "hid", [(0, 1), (1, 0)])


def swap_row(array, bit):
    return lax.ppermute(array, "row", [(i, i ^ bit) for i in range(lax.axis_size("row"))])


def after(array, *earlier):
    return lax.optimization_barrier((array, *earlier))[0]


def gather(w_up, b_up, w_down):
    number, me = lax.axis_size("hid"), lax.axis_index("hid")
    arrays = [lax.all_gather(a, "hid") for a in (w_up, b_up.reshape(1, -1), w_down)]
    pick = lambda a, k: lax.dynamic_index_in_dim(a, lax.rem(me + k, number), 0, keepdims=False)
    return [pick(a, k) for k in range(1, number) for a in arrays]


def shards(features, dw_weight, dw_bias, ln_gain, ln_bias, w_up, b_up, w_down, b_down, layer_scale):
    layout = Layout(features, dw_weight)
    blocks, rows, number = layout.blocks, layout.rows, layout.number
    me, row, count = lax.axis_index("hid"), lax.axis_index("row"), lax.axis_size("row")
    odd = lax.rem(row, 2)
    pairs = number == 2 and w_up.shape[2] == 2 * layout.channels and count % 8 == 0
    weights = (w_up, b_up, w_down)
    norm, ending = (ln_gain, ln_bias), (b_down, layer_scale)

    outer, inner, *packed = prepare(layout, features, weights if pairs else ())
    far, near = across(outer), within(inner)
    state = features
    if pairs:
        up, down = swap_hid(packed[0]), swap_hid(packed[1])
    for b in range(blocks):
        before, *complete = conv_own(b, layout, state, near, dw_weight, dw_bias)
        if not pairs:
            kind, parts = "plain", gather(w_up[b], b_up[b], w_down[b])
        if b < blocks - 1:
            if pairs:
                later = swap_hid(pack(b + 1, layout, weights))
            if pairs and b == 0:
                down = after(down, before)
                up_other, down_other = swap_row(up, 4), swap_row(down, 4)
            chosen = layout.result_rows(b)
            x, total = conv_rest(b, layout, chosen, far, before, dw_weight, *norm, weights)
            if pairs and b == 0:
                up_other, down_other = after(up_other, total), after(down_other, total)
                mine = [up, down, up_other, down_other]
                kind, parts = "pairs", [within(a) for a in mine]
                biases = mine[::2], parts[::2]
                total = add(b, layout, x, total, kind, mine)
            elif pairs:
                kind, parts = "joined", [joined, *biases[0], within(joined), *biases[1]]
            state, outer, inner = more(
                b, layout, chosen, x, (total,), kind, parts, state, *ending, far
            )
            far, near = across(outer), within(inner)
            if pairs:
                joined = later
            continue
        first, last = tuple(range(before.shape[1])), tuple(range(before.shape[1], rows))
        x, total = conv_rest(b, layout, last, None, complete[0], dw_weight, *norm, weights)
        rest = None if pairs else parts
        if pairs and b == 0:
            kind, parts = "plain", gather(w_up[b], b_up[b], w_down[b])
            rest = parts
        elif pairs:
            joined = after(joined, total)
            kind, rest = "joined", [within(joined), *biases[1]]
            here = [joined, *biases[0]]
            parts = here + rest
            total = add(b, layout, x, total, kind, here)
        before = after(before, total)
        x_first, = conv_rest(b, layout, first, far, before, dw_weight, *norm)
        total = after(total, x_first)
        inner, = more(b, layout, last, x, (total,), kind, rest, state, *ending)
        outer, = more(b, layout, first, x_first, weights, kind, parts, state, *ending)
    if number == 2:
        later = swap_hid(inner), swap_hid(outer)
        out = assemble(layout, None, [(inner, 0, 0), (outer, 1, 0), (later[0], 0, 1)])
        return assemble(layout, out, [(later[1], 1, 1)])
    if number > 2:
        inner, outer = (lax.all_gather(a, "hid", axis=1, tiled=True) for a in (inner, outer))
    if inner.shape == outer.shape:
        return jnp.concatenate([jnp.where(odd == 1, inner, outer), jnp.where(odd == 1, outer, inner)])
    return jnp.where(odd == 1, jnp.concatenate([inner, outer]), jnp.concatenate([outer, inner]))


def solution(mesh):
    return jax.shard_map(
        shards,
        mesh=mesh,
        in_specs=(
            P("row", None, None),
            P(),
            P(),
            P(),
            P(),
            P(None, None, "hid"),
            P(None, "hid"),
            P(None, "hid", None),
            P(),
            P(),
        ),
        out_specs=P("row", None, None),
        check_vma=False,
    )
```

```python
import functools

import jax
import jax.numpy as jnp
from jax import lax
from jax.experimental import pallas as pl
from jax.experimental.pallas import tpu as pltpu
from jax.sharding import PartitionSpec as P

LANES = 128
MARGIN = 16
LONG = 10**11
ERF = (
    0.7978275766866006,
    0.036469930744144466,
    -0.00012547620415072412,
    -3.0467196783772113e-05,
    1.1126315774795922e-06,
)
VMEM = pl.BlockSpec(memory_space=pltpu.VMEM)
HBM = pl.BlockSpec(memory_space=pltpu.HBM)
PARAMS = pltpu.CompilerParams(vmem_limit_bytes=20 * 1024 * 1024)
COPIES = pltpu.CompilerParams(vmem_limit_bytes=61 * 1024 * 1024)


def twice_gelu(u):
    v = u * u
    p = jnp.full_like(u, ERF[-1])
    for c in ERF[-2::-1]:
        p = p * v + c
    return u + u * jnp.tanh(u * p)


def tile_of(width):
    return next(s for s in (72, 64, 48, 32, 16) if width % s == 0)


class Layout:
    def __init__(self, features, kernels):
        self.blocks, self.reach = kernels.shape[0], kernels.shape[1] // 2
        self.rows, self.columns, self.channels = features.shape
        self.number = lax.axis_size("hid")
        self.width = self.columns // self.number

    def size(self, reach, unit):
        extra = -(-reach // unit) * unit
        return extra, min(self.columns, self.width + (1 if self.number == 2 else 2) * extra)

    def start(self, reach, unit):
        extra, size = self.size(reach, unit)
        return jnp.clip(lax.axis_index("hid") * self.width - extra, 0, self.columns - size)

    def window(self, b):
        return self.reach * (self.blocks - 1 - b), MARGIN

    def edge(self, b):
        return self.reach * (self.blocks - b), 8 if b else MARGIN

    def extra(self, b):
        same = self.size(*self.window(0)) == self.size(*self.edge(0))
        return int(b == 0 and self.blocks > 1 and self.rows > self.reach and same)

    def own_rows(self, b):
        return range(-self.extra(b - 1), self.rows)

    def result_rows(self, b):
        return range(-self.extra(b), self.rows)

    def far_rows(self, b):
        return range(self.extra(b - 1), self.reach + self.extra(b))

    def place(self, b):
        to, halo = self.start(*self.window(b)), self.start(*self.edge(b))
        start = self.start(*self.window(b - 1)) if b else 0
        later = self.start(*self.edge(b + 1))
        row = lax.axis_index("row")
        odd, parity = lax.rem(row, 2), lax.rem(lax.div(row, 4), 2)
        there = jnp.where(odd == 1, row < lax.axis_size("row") - 1, row > 0)
        return to - start, halo - to + MARGIN, odd, parity, there, later - to, halo


def own_row(layout, b, place, d):
    return d + layout.extra(b - 1) if b else jnp.where(place[2] == 1, layout.rows - 1 - d, d)


def far_row(layout, b, place, k):
    rows = layout.far_rows(b)
    return k - rows[0] if b else jnp.where(place[2] == 1, k, len(rows) - 1 - k)


def tap_of(place, t, size):
    return jnp.where(place[2] == 1, size - 1 - t, t)


def convolve(b, place, sums, wide, inputs, outputs, taps, c, lanes, start, step):
    size = taps.shape[1]
    reach = size // 2
    for i, position in enumerate(inputs):
        used = [(n, position - d + reach) for n, d in enumerate(outputs)]
        used = [(n, tap_of(place, t, size)) for n, t in used if 0 <= t < size]
        if not used:
            continue
        for j in range(size):
            first = start + MARGIN + j - reach
            x = wide[c, i, first : first + step]
            for n, t in used:
                sums[n] = sums[n] + x * taps[b, t, j : j + 1, lanes]
    return sums


def own_kernel(b, layout, complete, own, near, taps, bias, *refs):
    place = layout.place(b)
    out, *conv, wide = refs
    groups, _, width, _ = out.shape
    reach = near.shape[0]
    rows, outputs = layout.own_rows(b), layout.result_rows(b)
    fill_own(layout, b, place, own, wide)
    back = place[2] if b == 0 else 1
    sources = [(near, jnp.where(back == 1, reach - 1 - k, k)) for k in range(reach)]
    fill_halo(place, sources, wide, len(rows))
    step = tile_of(width)
    inputs = range(rows[0], layout.rows + reach)

    def group(c, _):
        lanes = pl.ds(pl.multiple_of(c * LANES, LANES), LANES)
        for start in range(0, width, step):
            sums = [jnp.broadcast_to(bias[b : b + 1, lanes], (step, LANES)) for _ in outputs]
            sums = convolve(b, place, sums, wide, inputs, outputs, taps, c, lanes, start, step)
            for n, d in enumerate(outputs):
                if d in complete:
                    conv[0][c, d - complete[0], start : start + step] = sums[n]
                else:
                    out[c, n, start : start + step] = sums[n]
        return 0

    lax.fori_loop(0, groups, group, 0)


def fill_own(layout, b, place, own, wide):
    groups, _, columns, _ = wide.shape
    for k in range(columns // MARGIN):
        at = place[0] + (k - 1) * MARGIN
        inside = (at >= 0) & (at <= own.shape[1] - MARGIN)
        at = pl.multiple_of(jnp.clip(at, 0, own.shape[1] - MARGIN), MARGIN)
        for n, d in enumerate(layout.own_rows(b)):
            for c in range(groups):
                x = own[own_row(layout, b, place, d), pl.ds(at, MARGIN), c * LANES : (c + 1) * LANES]
                x = jnp.where(inside, x.astype(jnp.float32), 0.0)
                wide[c, n, k * MARGIN : (k + 1) * MARGIN] = x


def fill_halo(place, sources, wide, first):
    groups, _, columns, _ = wide.shape
    size = sources[0][0].shape[1]
    at = pl.ds(pl.multiple_of(place[1], 8), size)
    for i, (ref, row) in enumerate(sources):
        for c in range(groups):
            zeros = jnp.zeros((2 * MARGIN, LANES), jnp.float32)
            wide[c, first + i, : 2 * MARGIN] = zeros
            wide[c, first + i, columns - 2 * MARGIN :] = zeros
            x = ref[row, :, c * LANES : (c + 1) * LANES].astype(jnp.float32)
            wide[c, first + i, at] = x


def add_far(b, layout, place, chosen, far, before, taps, conv, wide):
    groups, _, width, _ = before.shape
    rows = layout.far_rows(b)
    fill_halo(place, [(far, far_row(layout, b, place, k)) for k in rows], wide, 0)
    step = tile_of(width)
    inputs = [-1 - k for k in rows]

    def group(c, _):
        lanes = pl.ds(pl.multiple_of(c * LANES, LANES), LANES)
        for start in range(0, width, step):
            sums = [before[c, n, start : start + step] for n in range(len(chosen))]
            sums = convolve(b, place, sums, wide, inputs, chosen, taps, c, lanes, start, step)
            for n in range(len(chosen)):
                conv[c, n, start : start + step] = sums[n]
        return 0

    lax.fori_loop(0, groups, group, 0)


def normalise(b, conv, gain, shift, out):
    groups, rows, width, _ = conv.shape
    channels = groups * LANES
    for r in range(rows):
        x = [conv[c, r].astype(jnp.bfloat16).astype(jnp.float32) for c in range(groups)]
        mean = jnp.sum(functools.reduce(jnp.add, x), axis=1, keepdims=True) * (1.0 / channels)
        x = [v - mean for v in x]
        var = jnp.sum(functools.reduce(jnp.add, [v * v for v in x]), axis=1, keepdims=True)
        scale = lax.rsqrt(var * (1.0 / channels) + 1e-06)
        for c in range(groups):
            lanes = slice(c * LANES, (c + 1) * LANES)
            y = x[c] * scale * gain[b : b + 1, lanes] + shift[b : b + 1, lanes]
            out[r * width : (r + 1) * width, lanes] = y.astype(out.dtype)


def project(x, up, b_up, down, total, before=None):
    hidden = down.shape[0]
    part = 256 if hidden % 256 == 0 else 128
    for k in range(0, hidden, part):
        u = jnp.dot(x[...], up[:, k : k + part], preferred_element_type=jnp.float32)
        h = twice_gelu(u + b_up[:, k : k + part]).astype(jnp.bfloat16)
        y = jnp.dot(h, down[k : k + part, :], preferred_element_type=jnp.float32)
        if k:
            total[...] += y
        else:
            total[...] = y if before is None else before[...] + y


def rest_kernel(b, layout, chosen, whole, *refs):
    place = layout.place(b)
    refs = list(refs)
    far = refs.pop(0) if chosen[0] < layout.reach - layout.extra(b - 1) else None
    before, gain, shift, *refs = refs
    if far is None:
        conv = before
    else:
        taps, *refs, conv, wide = refs
        add_far(b, layout, place, chosen, far, before, taps, conv, wide)
    if whole:
        up, b_up, down, normed, total = refs
        normalise(b, conv, gain, shift, normed)
        project(normed, up.at[b], b_up.at[b : b + 1], down.at[b], total)
    else:
        normalise(b, conv, gain, shift, refs[0])


def pieces_of(kind, layout, b, parts):
    channels = layout.channels
    if kind == "plain":
        return [(parts[n], parts[n + 1][...], parts[n + 2]) for n in range(0, len(parts), 3)]

    def bias(part):
        terms = part[channels:, :].astype(jnp.float32)
        return terms[2 * b : 2 * b + 1] + terms[2 * b + 1 : 2 * b + 2]

    if kind == "pairs":
        return [(p.at[:channels], bias(p), q) for p, q in zip(parts[::2], parts[1::2])]
    pieces, parity = [], layout.place(b)[3]
    for part, mine, other in zip(parts[::3], parts[1::3], parts[2::3]):
        mine, other = bias(mine), bias(other)
        halves = jnp.where(parity == 0, mine, other), jnp.where(parity == 0, other, mine)
        half = mine.shape[1]
        for n in range(2):
            columns = slice(n * half, (n + 1) * half)
            down = part.at[channels + n * half : channels + (n + 1) * half]
            pieces.append((part.at[:channels, columns], halves[n], down))
    return pieces


def add_kernel(b, layout, kind, x, before, *refs):
    for piece in pieces_of(kind, layout, b, refs[:-1]):
        project(x, *piece, refs[-1], before)
        before = refs[-1]


def more_kernel(b, layout, chosen, kind, number, begun, x, *refs):
    place = layout.place(b)
    final = b == layout.blocks - 1
    refs = list(refs)
    take = lambda count: [refs.pop(0) for _ in range(count)]
    pieces, first = [], None
    if begun:
        first = refs.pop(0)
    else:
        up, b_up, down = take(3)
        pieces.append((up.at[b], b_up.at[b : b + 1], down.at[b]))
    parts = take(number)
    state, b_down, scale = take(3)
    far_state = None if final else refs.pop(0)
    out = refs.pop(0)
    sends = [] if final else take(2)
    total = refs.pop(0)
    pieces += pieces_of(kind, layout, b, parts)
    for piece in pieces:
        project(x, *piece, total, first)
        first = total
    count, width, _ = out.shape
    rows, reach = layout.rows, layout.reach
    for n, d in enumerate(chosen):
        if d < 0:
            s = far_state[far_row(layout, b, place, -1 - d), :, :].astype(jnp.float32)
        else:
            at = pl.ds(pl.multiple_of(place[0], MARGIN), width)
            s = state[own_row(layout, b, place, d), at, :].astype(jnp.float32)
        y = 0.5 * first[n * width : (n + 1) * width, :] + b_down[b : b + 1]
        s = s + scale[b : b + 1] * y
        if final:
            out[jnp.where(place[2] == 1, count - 1 - n, n)] = s.astype(out.dtype)
            continue
        if d < 0:
            s = jnp.where(place[4], s, 0.0)
        out[n] = s.astype(out.dtype)
        total[n * width : (n + 1) * width, :] = s
        far, near = sends
        size = near.shape[1]
        s = total[pl.ds(pl.multiple_of(n * width + place[5], 8), size), :].astype(out.dtype)
        if d in layout.far_rows(b + 1):
            far[d - layout.far_rows(b + 1)[0]] = s
        if d >= rows - reach:
            near[d - (rows - reach)] = s


def take(b, place, weights, parts, up, down):
    w_up, w_down = weights
    hidden = w_up.shape[2] // parts
    at = place[2] * (w_up.shape[2] // 2) + (place[3] * hidden if parts == 4 else 0)
    at = pl.ds(pl.multiple_of(at, hidden), hidden)
    return at, [(w_up.at[b, :, at], up), (w_down.at[b, at, :], down)]


def in_two_terms(value, terms, first=0):
    high = value.astype(jnp.bfloat16).astype(jnp.float32)
    low = (value - high).astype(jnp.bfloat16).astype(jnp.float32)
    row = lax.broadcasted_iota(jnp.int32, terms.shape, 0)
    rest = terms[...].astype(jnp.float32) if first else 0.0
    both = jnp.where(row == first, high, jnp.where(row == first + 1, low, rest))
    terms[...] = both.astype(terms.dtype)


def start(copies, sems):
    copies = [pltpu.make_async_copy(*copy, sems.at[n]) for n, copy in enumerate(copies)]
    for copy in copies:
        copy.start()
    return copies


def prepare_kernel(layout, features, *refs):
    place = layout.place(0)
    weights, refs = refs[: 3 if len(refs) > 5 else 0], refs[3 if len(refs) > 5 else 0 :]
    *refs, sems = refs
    if weights:
        *refs, bias, terms = refs
    outs, stages = list(refs[: len(refs) // 2]), list(refs[len(refs) // 2 :])
    at = pl.ds(pl.multiple_of(place[6], MARGIN), outs[0].shape[1])
    sources = []
    for side, out in zip((place[2], 1 - place[2]), outs):
        count = out.shape[0]
        sources.append(features.at[pl.ds(side * (layout.rows - count), count), at])
    if outs[0].shape[0] == layout.rows:
        sources.pop()
    if weights:
        channels = layout.channels
        hidden, taken = take(0, place, weights[::2], 4, stages[2].at[:channels], stages[3])
        first = start([*taken, (weights[1], bias)], sems.at[0])
        rest = start(list(zip(sources, stages)), sems.at[1])
        first[2].wait()
        for b in range(layout.blocks):
            in_two_terms(bias[b : b + 1, hidden], terms, 2 * b)
        first[0].wait()
        legs = [(stages[2].at[:channels], outs[2].at[:channels]), (terms, outs[2].at[channels:])]
        legs = start(legs, sems.at[2])
        first[1].wait()
        legs += start([(stages[3], outs[3])], sems.at[3])
    else:
        rest = start(list(zip(sources, stages)), sems.at[1])
        legs = []
    rest[0].wait()
    if outs[0].shape[0] == layout.rows:
        inner = stages[0].at[pl.ds((1 - place[2]) * (layout.rows - layout.reach), layout.reach)]
    else:
        rest[1].wait()
        inner = stages[1]
    legs += start([(stages[0], outs[0]), (inner, outs[1])], sems.at[4])
    for copy in legs:
        copy.wait()


def pack_kernel(b, layout, w_up, w_down, out, sems):
    channels = layout.channels
    copies = take(b, layout.place(b), (w_up, w_down), 2, out.at[:channels], out.at[channels:])[1]
    for copy in start(copies, sems):
        copy.wait()


def cost(flops):
    return pl.CostEstimate(flops=flops, bytes_accessed=0, transcendentals=0)


def prepare(layout, features, weights=()):
    _, size = layout.size(*layout.edge(0))
    channels = layout.channels
    shapes = [(count, size, channels) for count in (len(layout.far_rows(0)), layout.reach)]
    scratch = [pltpu.SemaphoreType.DMA((6, 3))]
    if weights:
        hidden = weights[0].shape[2] // 4
        shapes += [(channels + MARGIN, hidden), (hidden, channels)]
        scratch.insert(0, pltpu.VMEM((MARGIN, hidden), jnp.bfloat16))
        scratch.insert(0, pltpu.VMEM(weights[1].shape, jnp.float32))
    return pl.pallas_call(
        functools.partial(prepare_kernel, layout),
        out_shape=[jax.ShapeDtypeStruct(shape, jnp.bfloat16) for shape in shapes],
        in_specs=[HBM] + [HBM] * len(weights),
        out_specs=[HBM] * len(shapes),
        scratch_shapes=[pltpu.VMEM(shape, jnp.bfloat16) for shape in shapes] + scratch,
        compiler_params=COPIES,
        cost_estimate=cost(1),
        name="prepare",
    )(features, *weights)


def pack(b, layout, weights):
    _, channels, hidden = weights[0].shape
    shape = (channels + hidden // 2, channels)
    return pl.pallas_call(
        functools.partial(pack_kernel, b, layout),
        out_shape=jax.ShapeDtypeStruct(shape, jnp.bfloat16),
        in_specs=[HBM, HBM],
        out_specs=VMEM,
        scratch_shapes=[pltpu.SemaphoreType.DMA((2,))],
        compiler_params=PARAMS,
        cost_estimate=cost(1),
        name="pack",
    )(*weights[::2])


def conv_own(b, layout, own, near, taps, bias):
    groups = layout.channels // LANES
    _, width = layout.size(*layout.window(b))
    final = b == layout.blocks - 1
    complete = range(layout.reach - layout.extra(b - 1), layout.rows) if final else range(0)
    counts = [len(layout.result_rows(b)) - len(complete)] + [len(complete)] * final
    lines = len(layout.own_rows(b)) + layout.reach
    return pl.pallas_call(
        functools.partial(own_kernel, b, layout, complete),
        out_shape=[jax.ShapeDtypeStruct((groups, n, width, LANES), jnp.float32) for n in counts],
        in_specs=[VMEM] * 4,
        out_specs=[VMEM] * len(counts),
        scratch_shapes=[pltpu.VMEM((groups, lines, width + 2 * MARGIN, LANES), jnp.float32)],
        compiler_params=PARAMS,
        cost_estimate=cost(1 if final else LONG),
        name="conv_own",
    )(own, near, taps, bias)


def conv_rest(b, layout, chosen, far, before, taps, gain, shift, weights=()):
    groups, rows, width, _ = before.shape
    channels = layout.channels
    args = [before, gain, shift]
    shapes = [jax.ShapeDtypeStruct((rows * width, channels), jnp.bfloat16)]
    scratch = []
    if far is not None:
        args = [far, *args, taps]
        lines = len(layout.far_rows(b))
        scratch.append(pltpu.VMEM((groups, rows, width, LANES), jnp.float32))
        scratch.append(pltpu.VMEM((groups, lines, width + 2 * MARGIN, LANES), jnp.float32))
    if weights:
        args += weights
        shapes.append(jax.ShapeDtypeStruct((rows * width, channels), jnp.float32))
    return pl.pallas_call(
        functools.partial(rest_kernel, b, layout, chosen, bool(weights)),
        out_shape=shapes,
        in_specs=[VMEM] * len(args),
        out_specs=[VMEM] * len(shapes),
        scratch_shapes=scratch,
        compiler_params=PARAMS,
        cost_estimate=cost(1 if weights else LONG),
        name="conv_rest",
    )(*args)


def add(b, layout, x, before, kind, parts):
    return pl.pallas_call(
        functools.partial(add_kernel, b, layout, kind),
        out_shape=jax.ShapeDtypeStruct(before.shape, jnp.float32),
        in_specs=[VMEM] * (2 + len(parts)),
        out_specs=VMEM,
        compiler_params=PARAMS,
        cost_estimate=cost(1),
        name="add",
    )(x, before, *parts)


def more(b, layout, chosen, x, begun, kind, parts, state, b_down, scale, far=None):
    positions, channels = x.shape
    args = [x, *begun, *parts, state, b_down, scale]
    shapes = [(len(chosen), positions // len(chosen), channels)]
    if far is not None:
        args.append(far)
        _, size = layout.size(*layout.edge(b + 1))
        shapes += [(n, size, channels) for n in (len(layout.far_rows(b + 1)), layout.reach)]
    return pl.pallas_call(
        functools.partial(more_kernel, b, layout, chosen, kind, len(parts), len(begun) == 1),
        out_shape=[jax.ShapeDtypeStruct(shape, jnp.bfloat16) for shape in shapes],
        in_specs=[VMEM] * len(args),
        out_specs=[VMEM] * len(shapes),
        scratch_shapes=[pltpu.VMEM((positions, channels), jnp.float32)],
        compiler_params=PARAMS,
        cost_estimate=cost(1),
        name="more",
    )(*args)


def assemble_kernel(layout, kinds, *refs):
    *parts, out, sems = refs
    parts = parts[len(parts) - len(kinds) :]
    _, _, odd, *_ = layout.place(layout.blocks - 1)
    copies = []
    for part, (outer, other) in zip(parts, kinds):
        count = part.shape[0]
        row = jnp.where(odd == outer, layout.rows - count, 0)
        me = lax.axis_index("hid")
        column = pl.multiple_of((1 - me if other else me) * layout.width, MARGIN)
        copies.append((part, out.at[pl.ds(row, count), pl.ds(column, layout.width)]))
    for copy in start(copies, sems):
        copy.wait()


def assemble(layout, out, parts):
    anywhere = pl.BlockSpec(memory_space=pl.ANY)
    shape = (layout.rows, layout.columns, layout.channels)
    args = ([] if out is None else [out]) + [part for part, *_ in parts]
    return pl.pallas_call(
        functools.partial(assemble_kernel, layout, [kind for _, *kind in parts]),
        out_shape=jax.ShapeDtypeStruct(shape, jnp.bfloat16),
        in_specs=([] if out is None else [anywhere]) + [VMEM] * len(parts),
        out_specs=anywhere,
        scratch_shapes=[pltpu.SemaphoreType.DMA((len(parts),))],
        input_output_aliases={} if out is None else {0: 0},
        compiler_params=PARAMS,
        cost_estimate=cost(1),
        name="assemble",
    )(*args)


def within(array):
    return lax.ppermute(array, "row", [(i, i ^ 1) for i in range(lax.axis_size("row"))])


def across(array):
    pairs = [(i, i + 1) for i in range(1, lax.axis_size("row") - 1, 2)]
    return lax.ppermute(array, "row", pairs + [(target, source) for source, target in pairs])


def swap_hid(array):
    return lax.ppermute(array, "hid", [(0, 1), (1, 0)])


def swap_row(array, bit):
    return lax.ppermute(array, "row", [(i, i ^ bit) for i in range(lax.axis_size("row"))])


def after(array, *earlier):
    return lax.optimization_barrier((array, *earlier))[0]


def gather(w_up, b_up, w_down):
    number, me = lax.axis_size("hid"), lax.axis_index("hid")
    arrays = [lax.all_gather(a, "hid") for a in (w_up, b_up.reshape(1, -1), w_down)]
    pick = lambda a, k: lax.dynamic_index_in_dim(a, lax.rem(me + k, number), 0, keepdims=False)
    return [pick(a, k) for k in range(1, number) for a in arrays]


def shards(features, dw_weight, dw_bias, ln_gain, ln_bias, w_up, b_up, w_down, b_down, layer_scale):
    layout = Layout(features, dw_weight)
    blocks, rows, number = layout.blocks, layout.rows, layout.number
    me, row, count = lax.axis_index("hid"), lax.axis_index("row"), lax.axis_size("row")
    odd = lax.rem(row, 2)
    pairs = number == 2 and w_up.shape[2] == 2 * layout.channels and count % 8 == 0
    weights = (w_up, b_up, w_down)
    norm, ending = (ln_gain, ln_bias), (b_down, layer_scale)

    outer, inner, *packed = prepare(layout, features, weights if pairs else ())
    far, near = across(outer), within(inner)
    state = features
    if pairs:
        up, down = swap_hid(packed[0]), swap_hid(packed[1])
    for b in range(blocks):
        before, *complete = conv_own(b, layout, state, near, dw_weight, dw_bias)
        if not pairs:
            kind, parts = "plain", gather(w_up[b], b_up[b], w_down[b])
        if b < blocks - 1:
            if pairs:
                later = swap_hid(pack(b + 1, layout, weights))
            if pairs and b == 0:
                down = after(down, before)
                up_other, down_other = swap_row(up, 4), swap_row(down, 4)
            chosen = layout.result_rows(b)
            x, total = conv_rest(b, layout, chosen, far, before, dw_weight, *norm, weights)
            if pairs and b == 0:
                up_other, down_other = after(up_other, total), after(down_other, total)
                mine = [up, down, up_other, down_other]
                kind, parts = "pairs", [within(a) for a in mine]
                biases = mine[::2], parts[::2]
                total = add(b, layout, x, total, kind, mine)
            elif pairs:
                kind, parts = "joined", [joined, *biases[0], within(joined), *biases[1]]
            state, outer, inner = more(
                b, layout, chosen, x, (total,), kind, parts, state, *ending, far
            )
            far, near = across(outer), within(inner)
            if pairs:
                joined = later
            continue
        first, last = tuple(range(before.shape[1])), tuple(range(before.shape[1], rows))
        x, total = conv_rest(b, layout, last, None, complete[0], dw_weight, *norm, weights)
        rest = None if pairs else parts
        if pairs and b == 0:
            kind, parts = "plain", gather(w_up[b], b_up[b], w_down[b])
            rest = parts
        elif pairs:
            joined = after(joined, total)
            kind, rest = "joined", [within(joined), *biases[1]]
            here = [joined, *biases[0]]
            parts = here + rest
            total = add(b, layout, x, total, kind, here)
        before = after(before, total)
        x_first, = conv_rest(b, layout, first, far, before, dw_weight, *norm)
        total = after(total, x_first)
        inner, = more(b, layout, last, x, (total,), kind, rest, state, *ending)
        outer, = more(b, layout, first, x_first, weights, kind, parts, state, *ending)
    if number == 2:
        later = swap_hid(inner), swap_hid(outer)
        out = assemble(layout, None, [(inner, 0, 0), (outer, 1, 0), (later[0], 0, 1)])
        return assemble(layout, out, [(later[1], 1, 1)])
    if number > 2:
        inner, outer = (lax.all_gather(a, "hid", axis=1, tiled=True) for a in (inner, outer))
    if inner.shape == outer.shape:
        return jnp.concatenate([jnp.where(odd == 1, inner, outer), jnp.where(odd == 1, outer, inner)])
    return jnp.where(odd == 1, jnp.concatenate([inner, outer]), jnp.concatenate([outer, inner]))


def solution(mesh):
    return jax.shard_map(
        shards,
        mesh=mesh,
        in_specs=(
            P("row", None, None),
            P(),
            P(),
            P(),
            P(),
            P(None, None, "hid"),
            P(None, "hid"),
            P(None, "hid", None),
            P(),
            P(),
        ),
        out_specs=P("row", None, None),
        check_vma=False,
    )
```

```python
import functools

import jax
import jax.numpy as jnp
from jax import lax
from jax.experimental import pallas as pl
from jax.experimental.pallas import tpu as pltpu
from jax.sharding import PartitionSpec as P

LANES = 128
MARGIN = 16
LONG = 10**11
ERF = (
    0.7978275766866006,
    0.036469930744144466,
    -0.00012547620415072412,
    -3.0467196783772113e-05,
    1.1126315774795922e-06,
)
VMEM = pl.BlockSpec(memory_space=pltpu.VMEM)
HBM = pl.BlockSpec(memory_space=pltpu.HBM)
PARAMS = pltpu.CompilerParams(vmem_limit_bytes=20 * 1024 * 1024)
COPIES = pltpu.CompilerParams(vmem_limit_bytes=61 * 1024 * 1024)


def twice_gelu(u):
    v = u * u
    p = jnp.full_like(u, ERF[-1])
    for c in ERF[-2::-1]:
        p = p * v + c
    return u + u * jnp.tanh(u * p)


def tile_of(width):
    return next(s for s in (72, 64, 48, 32, 16) if width % s == 0)


class Layout:
    def __init__(self, features, kernels):
        self.blocks, self.reach = kernels.shape[0], kernels.shape[1] // 2
        self.rows, self.columns, self.channels = features.shape
        self.number = lax.axis_size("hid")
        self.width = self.columns // self.number

    def size(self, reach, unit):
        extra = -(-reach // unit) * unit
        return extra, min(self.columns, self.width + (1 if self.number == 2 else 2) * extra)

    def start(self, reach, unit):
        extra, size = self.size(reach, unit)
        return jnp.clip(lax.axis_index("hid") * self.width - extra, 0, self.columns - size)

    def window(self, b):
        return self.reach * (self.blocks - 1 - b), MARGIN

    def edge(self, b):
        return self.reach * (self.blocks - b), 8

    def extra(self, b):
        return int(b == 0 and self.blocks > 1 and self.rows > self.reach)

    def own_rows(self, b):
        return range(-self.extra(b - 1), self.rows)

    def result_rows(self, b):
        return range(-self.extra(b), self.rows)

    def far_rows(self, b):
        return range(self.extra(b - 1), self.reach + self.extra(b))

    def place(self, b):
        to, halo = self.start(*self.window(b)), self.start(*self.edge(b))
        start = self.start(*self.window(b - 1)) if b else 0
        later = self.start(*self.edge(b + 1))
        row = lax.axis_index("row")
        odd, parity = lax.rem(row, 2), lax.rem(lax.div(row, 4), 2)
        there = jnp.where(odd == 1, row < lax.axis_size("row") - 1, row > 0)
        return to - start, halo - to + MARGIN, odd, parity, there, later - to, halo


def own_row(layout, b, place, d):
    return d + layout.extra(b - 1) if b else jnp.where(place[2] == 1, layout.rows - 1 - d, d)


def far_row(layout, b, place, k):
    rows = layout.far_rows(b)
    return k - rows[0] if b else jnp.where(place[2] == 1, k, len(rows) - 1 - k)


def tap_of(place, t, size):
    return jnp.where(place[2] == 1, size - 1 - t, t)


def convolve(b, place, sums, wide, inputs, outputs, taps, c, lanes, start, step):
    size = taps.shape[1]
    reach = size // 2
    for i, position in enumerate(inputs):
        used = [(n, position - d + reach) for n, d in enumerate(outputs)]
        used = [(n, tap_of(place, t, size)) for n, t in used if 0 <= t < size]
        if not used:
            continue
        for j in range(size):
            first = start + MARGIN + j - reach
            x = wide[c, i, first : first + step]
            for n, t in used:
                sums[n] = sums[n] + x * taps[b, t, j : j + 1, lanes]
    return sums


def own_kernel(b, layout, complete, own, near, taps, bias, *refs):
    place = layout.place(b)
    out, *conv, wide = refs
    groups, _, width, _ = out.shape
    reach = near.shape[0]
    rows, outputs = layout.own_rows(b), layout.result_rows(b)
    fill_own(layout, b, place, own, wide)
    back = place[2] if b == 0 else 1
    sources = [(near, jnp.where(back == 1, reach - 1 - k, k)) for k in range(reach)]
    fill_halo(place, sources, wide, len(rows))
    step = tile_of(width)
    inputs = range(rows[0], layout.rows + reach)

    def group(c, _):
        lanes = pl.ds(pl.multiple_of(c * LANES, LANES), LANES)
        for start in range(0, width, step):
            sums = [jnp.broadcast_to(bias[b : b + 1, lanes], (step, LANES)) for _ in outputs]
            sums = convolve(b, place, sums, wide, inputs, outputs, taps, c, lanes, start, step)
            for n, d in enumerate(outputs):
                if d in complete:
                    conv[0][c, d - complete[0], start : start + step] = sums[n]
                else:
                    out[c, n, start : start + step] = sums[n]
        return 0

    lax.fori_loop(0, groups, group, 0)


def fill_own(layout, b, place, own, wide):
    groups, _, columns, _ = wide.shape
    for k in range(columns // MARGIN):
        at = place[0] + (k - 1) * MARGIN
        inside = (at >= 0) & (at <= own.shape[1] - MARGIN)
        at = pl.multiple_of(jnp.clip(at, 0, own.shape[1] - MARGIN), MARGIN)
        for n, d in enumerate(layout.own_rows(b)):
            for c in range(groups):
                x = own[own_row(layout, b, place, d), pl.ds(at, MARGIN), c * LANES : (c + 1) * LANES]
                x = jnp.where(inside, x.astype(jnp.float32), 0.0)
                wide[c, n, k * MARGIN : (k + 1) * MARGIN] = x


def fill_halo(place, sources, wide, first):
    groups, _, columns, _ = wide.shape
    size = sources[0][0].shape[1]
    at = pl.ds(pl.multiple_of(place[1], 8), size)
    for i, (ref, row) in enumerate(sources):
        for c in range(groups):
            zeros = jnp.zeros((2 * MARGIN, LANES), jnp.float32)
            wide[c, first + i, : 2 * MARGIN] = zeros
            wide[c, first + i, columns - 2 * MARGIN :] = zeros
            x = ref[row, :, c * LANES : (c + 1) * LANES].astype(jnp.float32)
            wide[c, first + i, at] = x


def add_far(b, layout, place, chosen, far, before, taps, conv, wide):
    groups, _, width, _ = before.shape
    rows = layout.far_rows(b)
    fill_halo(place, [(far, far_row(layout, b, place, k)) for k in rows], wide, 0)
    step = tile_of(width)
    inputs = [-1 - k for k in rows]

    def group(c, _):
        lanes = pl.ds(pl.multiple_of(c * LANES, LANES), LANES)
        for start in range(0, width, step):
            sums = [before[c, n, start : start + step] for n in range(len(chosen))]
            sums = convolve(b, place, sums, wide, inputs, chosen, taps, c, lanes, start, step)
            for n in range(len(chosen)):
                conv[c, n, start : start + step] = sums[n]
        return 0

    lax.fori_loop(0, groups, group, 0)


def normalise(b, conv, gain, shift, out):
    groups, rows, width, _ = conv.shape
    channels = groups * LANES
    for r in range(rows):
        x = [conv[c, r].astype(jnp.bfloat16).astype(jnp.float32) for c in range(groups)]
        mean = jnp.sum(functools.reduce(jnp.add, x), axis=1, keepdims=True) * (1.0 / channels)
        x = [v - mean for v in x]
        var = jnp.sum(functools.reduce(jnp.add, [v * v for v in x]), axis=1, keepdims=True)
        scale = lax.rsqrt(var * (1.0 / channels) + 1e-06)
        for c in range(groups):
            lanes = slice(c * LANES, (c + 1) * LANES)
            y = x[c] * scale * gain[b : b + 1, lanes] + shift[b : b + 1, lanes]
            out[r * width : (r + 1) * width, lanes] = y.astype(out.dtype)


def project(x, up, b_up, down, total, before=None):
    hidden = down.shape[0]
    part = 256 if hidden % 256 == 0 else 128
    for k in range(0, hidden, part):
        u = jnp.dot(x[...], up[:, k : k + part], preferred_element_type=jnp.float32)
        h = twice_gelu(u + b_up[:, k : k + part]).astype(jnp.bfloat16)
        y = jnp.dot(h, down[k : k + part, :], preferred_element_type=jnp.float32)
        if k:
            total[...] += y
        else:
            total[...] = y if before is None else before[...] + y


def rest_kernel(b, layout, chosen, whole, *refs):
    place = layout.place(b)
    refs = list(refs)
    far = refs.pop(0) if chosen[0] < layout.reach - layout.extra(b - 1) else None
    before, gain, shift, *refs = refs
    if far is None:
        conv = before
    else:
        taps, *refs, conv, wide = refs
        add_far(b, layout, place, chosen, far, before, taps, conv, wide)
    if whole:
        up, b_up, down, normed, total = refs
        normalise(b, conv, gain, shift, normed)
        project(normed, up.at[b], b_up.at[b : b + 1], down.at[b], total)
    else:
        normalise(b, conv, gain, shift, refs[0])


def pieces_of(kind, layout, b, parts):
    channels = layout.channels
    if kind == "plain":
        return [(parts[n], parts[n + 1][...], parts[n + 2]) for n in range(0, len(parts), 3)]

    def bias(part):
        terms = part[channels:, :].astype(jnp.float32)
        return terms[2 * b : 2 * b + 1] + terms[2 * b + 1 : 2 * b + 2]

    if kind == "pairs":
        return [(p.at[:channels], bias(p), q) for p, q in zip(parts[::2], parts[1::2])]
    pieces, parity = [], layout.place(b)[3]
    for part, mine, other in zip(parts[::3], parts[1::3], parts[2::3]):
        mine, other = bias(mine), bias(other)
        halves = jnp.where(parity == 0, mine, other), jnp.where(parity == 0, other, mine)
        half = mine.shape[1]
        for n in range(2):
            columns = slice(n * half, (n + 1) * half)
            down = part.at[channels + n * half : channels + (n + 1) * half]
            pieces.append((part.at[:channels, columns], halves[n], down))
    return pieces


def add_kernel(b, layout, kind, x, before, *refs):
    for piece in pieces_of(kind, layout, b, refs[:-1]):
        project(x, *piece, refs[-1], before)
        before = refs[-1]


def more_kernel(b, layout, chosen, kind, number, begun, x, *refs):
    place = layout.place(b)
    final, channels = b == layout.blocks - 1, layout.channels
    refs = list(refs)
    take = lambda count: [refs.pop(0) for _ in range(count)]
    pieces, first = [], None
    if begun:
        first = refs.pop(0)
    else:
        up, b_up, down = take(3)
        pieces.append((up.at[b], b_up.at[b : b + 1], down.at[b]))
    parts = take(number)
    state, b_down, scale = take(3)
    far_state = None if final else refs.pop(0)
    out = refs.pop(0)
    sends = [] if final else take(2)
    total = refs.pop(0)
    pieces += pieces_of(kind, layout, b, parts)
    for piece in pieces:
        project(x, *piece, total, first)
        first = total
    count, width, _ = out.shape
    rows, reach = layout.rows, layout.reach
    for n, d in enumerate(chosen):
        y = 0.5 * first[n * width : (n + 1) * width, :] + b_down[b : b + 1]
        if d < 0:
            total[n * width : (n + 1) * width, :] = jnp.zeros((width, channels), jnp.float32)
            at = pl.multiple_of(n * width + place[1] - MARGIN, 8)
            s = far_state[far_row(layout, b, place, -1 - d), :, :].astype(jnp.float32)
            total[pl.ds(at, far_state.shape[1]), :] = s
            s = total[n * width : (n + 1) * width, :]
        else:
            at = pl.ds(pl.multiple_of(place[0], MARGIN), width)
            s = state[own_row(layout, b, place, d), at, :].astype(jnp.float32)
        s = s + scale[b : b + 1] * y
        if final:
            out[jnp.where(place[2] == 1, count - 1 - n, n)] = s.astype(out.dtype)
            continue
        if d < 0:
            s = jnp.where(place[4], s, 0.0)
        out[n] = s.astype(out.dtype)
        total[n * width : (n + 1) * width, :] = s
        far, near = sends
        size = near.shape[1]
        s = total[pl.ds(pl.multiple_of(n * width + place[5], 8), size), :].astype(out.dtype)
        if d in layout.far_rows(b + 1):
            far[d - layout.far_rows(b + 1)[0]] = s
        if d >= rows - reach:
            near[d - (rows - reach)] = s


def take(b, place, weights, parts, up, down):
    w_up, w_down = weights
    hidden = w_up.shape[2] // parts
    at = place[2] * (w_up.shape[2] // 2) + (place[3] * hidden if parts == 4 else 0)
    at = pl.ds(pl.multiple_of(at, hidden), hidden)
    return at, [(w_up.at[b, :, at], up), (w_down.at[b, at, :], down)]


def in_two_terms(value, terms, first=0):
    high = value.astype(jnp.bfloat16).astype(jnp.float32)
    low = (value - high).astype(jnp.bfloat16).astype(jnp.float32)
    row = lax.broadcasted_iota(jnp.int32, terms.shape, 0)
    rest = terms[...].astype(jnp.float32) if first else 0.0
    both = jnp.where(row == first, high, jnp.where(row == first + 1, low, rest))
    terms[...] = both.astype(terms.dtype)


def start(copies, sems):
    copies = [pltpu.make_async_copy(*copy, sems.at[n]) for n, copy in enumerate(copies)]
    for copy in copies:
        copy.start()
    return copies


def prepare_kernel(layout, features, *refs):
    place = layout.place(0)
    weights, refs = refs[: 3 if len(refs) > 6 else 0], refs[3 if len(refs) > 6 else 0 :]
    *refs, stage, moved, row, sems = refs
    if weights:
        *refs, bias, terms = refs
        outs, stages = refs[:4], refs[4:]
    else:
        outs = refs
    begin = layout.start(layout.reach * layout.blocks, MARGIN)
    source = features.at[:, pl.ds(pl.multiple_of(begin, MARGIN), stage.shape[1])]
    legs = []
    if weights:
        channels = layout.channels
        hidden, taken = take(0, place, weights[::2], 4, stages[0].at[:channels], stages[1])
        first = start([*taken, (weights[1], bias)], sems.at[0])
    rest = start([(source, stage)], sems.at[1])
    if weights:
        first[2].wait()
        for b in range(layout.blocks):
            in_two_terms(bias[b : b + 1, hidden], terms, 2 * b)
        first[0].wait()
        legs = [(stages[0].at[:channels], outs[2].at[:channels]), (terms, outs[2].at[channels:])]
        legs = start(legs, sems.at[2])
        first[1].wait()
        legs += start([(stages[1], outs[3])], sems.at[3])
    rest[0].wait()
    at = pl.ds(pl.multiple_of(place[6] - begin, 8), moved.shape[1])
    for r in range(layout.rows):
        row[r] = stage[r].astype(jnp.float32)
        moved[r] = row[r, at, :].astype(moved.dtype)
    rows = []
    for side, out in zip((place[2], 1 - place[2]), outs):
        count = out.shape[0]
        rows.append((moved.at[pl.ds(side * (layout.rows - count), count)], out))
    for copy in legs + start(rows, sems.at[4]):
        copy.wait()


def pack_kernel(b, layout, w_up, w_down, out, sems):
    channels = layout.channels
    copies = take(b, layout.place(b), (w_up, w_down), 2, out.at[:channels], out.at[channels:])[1]
    for copy in start(copies, sems):
        copy.wait()


def cost(flops):
    return pl.CostEstimate(flops=flops, bytes_accessed=0, transcendentals=0)


def prepare(layout, features, weights=()):
    _, size = layout.size(*layout.edge(0))
    channels = layout.channels
    shapes = [(count, size, channels) for count in (len(layout.far_rows(0)), layout.reach)]
    _, wide = layout.size(layout.reach * layout.blocks, MARGIN)
    scratch = [
        pltpu.VMEM((layout.rows, wide, channels), jnp.bfloat16),
        pltpu.VMEM((layout.rows, size, channels), jnp.bfloat16),
        pltpu.VMEM((layout.rows, wide, channels), jnp.float32),
        pltpu.SemaphoreType.DMA((5, 3)),
    ]
    if weights:
        hidden = weights[0].shape[2] // 4
        more_shapes = [(channels + MARGIN, hidden), (hidden, channels)]
        shapes += more_shapes
        scratch = [
            *(pltpu.VMEM(shape, jnp.bfloat16) for shape in more_shapes),
            pltpu.VMEM(weights[1].shape, jnp.float32),
            pltpu.VMEM((MARGIN, hidden), jnp.bfloat16),
            *scratch,
        ]
    return pl.pallas_call(
        functools.partial(prepare_kernel, layout),
        out_shape=[jax.ShapeDtypeStruct(shape, jnp.bfloat16) for shape in shapes],
        in_specs=[HBM] + [HBM] * len(weights),
        out_specs=[HBM] * len(shapes),
        scratch_shapes=scratch,
        compiler_params=COPIES,
        cost_estimate=cost(1),
        name="prepare",
    )(features, *weights)


def pack(b, layout, weights):
    _, channels, hidden = weights[0].shape
    shape = (channels + hidden // 2, channels)
    return pl.pallas_call(
        functools.partial(pack_kernel, b, layout),
        out_shape=jax.ShapeDtypeStruct(shape, jnp.bfloat16),
        in_specs=[HBM, HBM],
        out_specs=VMEM,
        scratch_shapes=[pltpu.SemaphoreType.DMA((2,))],
        compiler_params=PARAMS,
        cost_estimate=cost(1),
        name="pack",
    )(*weights[::2])


def conv_own(b, layout, own, near, taps, bias):
    groups = layout.channels // LANES
    _, width = layout.size(*layout.window(b))
    final = b == layout.blocks - 1
    complete = range(layout.reach - layout.extra(b - 1), layout.rows) if final else range(0)
    counts = [len(layout.result_rows(b)) - len(complete)] + [len(complete)] * final
    lines = len(layout.own_rows(b)) + layout.reach
    return pl.pallas_call(
        functools.partial(own_kernel, b, layout, complete),
        out_shape=[jax.ShapeDtypeStruct((groups, n, width, LANES), jnp.float32) for n in counts],
        in_specs=[VMEM] * 4,
        out_specs=[VMEM] * len(counts),
        scratch_shapes=[pltpu.VMEM((groups, lines, width + 2 * MARGIN, LANES), jnp.float32)],
        compiler_params=PARAMS,
        cost_estimate=cost(1 if final else LONG),
        name="conv_own",
    )(own, near, taps, bias)


def conv_rest(b, layout, chosen, far, before, taps, gain, shift, weights=()):
    groups, rows, width, _ = before.shape
    channels = layout.channels
    args = [before, gain, shift]
    shapes = [jax.ShapeDtypeStruct((rows * width, channels), jnp.bfloat16)]
    scratch = []
    if far is not None:
        args = [far, *args, taps]
        lines = len(layout.far_rows(b))
        scratch.append(pltpu.VMEM((groups, rows, width, LANES), jnp.float32))
        scratch.append(pltpu.VMEM((groups, lines, width + 2 * MARGIN, LANES), jnp.float32))
    if weights:
        args += weights
        shapes.append(jax.ShapeDtypeStruct((rows * width, channels), jnp.float32))
    return pl.pallas_call(
        functools.partial(rest_kernel, b, layout, chosen, bool(weights)),
        out_shape=shapes,
        in_specs=[VMEM] * len(args),
        out_specs=[VMEM] * len(shapes),
        scratch_shapes=scratch,
        compiler_params=PARAMS,
        cost_estimate=cost(1 if weights else LONG),
        name="conv_rest",
    )(*args)


def add(b, layout, x, before, kind, parts):
    return pl.pallas_call(
        functools.partial(add_kernel, b, layout, kind),
        out_shape=jax.ShapeDtypeStruct(before.shape, jnp.float32),
        in_specs=[VMEM] * (2 + len(parts)),
        out_specs=VMEM,
        compiler_params=PARAMS,
        cost_estimate=cost(1),
        name="add",
    )(x, before, *parts)


def more(b, layout, chosen, x, begun, kind, parts, state, b_down, scale, far=None):
    positions, channels = x.shape
    args = [x, *begun, *parts, state, b_down, scale]
    shapes = [(len(chosen), positions // len(chosen), channels)]
    if far is not None:
        args.append(far)
        _, size = layout.size(*layout.edge(b + 1))
        shapes += [(n, size, channels) for n in (len(layout.far_rows(b + 1)), layout.reach)]
    return pl.pallas_call(
        functools.partial(more_kernel, b, layout, chosen, kind, len(parts), len(begun) == 1),
        out_shape=[jax.ShapeDtypeStruct(shape, jnp.bfloat16) for shape in shapes],
        in_specs=[VMEM] * len(args),
        out_specs=[VMEM] * len(shapes),
        scratch_shapes=[pltpu.VMEM((positions, channels), jnp.float32)],
        compiler_params=PARAMS,
        cost_estimate=cost(1),
        name="more",
    )(*args)


def assemble_kernel(layout, kinds, *refs):
    *parts, out, sems = refs
    parts = parts[len(parts) - len(kinds) :]
    _, _, odd, *_ = layout.place(layout.blocks - 1)
    copies = []
    for part, (outer, other) in zip(parts, kinds):
        count = part.shape[0]
        row = jnp.where(odd == outer, layout.rows - count, 0)
        me = lax.axis_index("hid")
        column = pl.multiple_of((1 - me if other else me) * layout.width, MARGIN)
        copies.append((part, out.at[pl.ds(row, count), pl.ds(column, layout.width)]))
    for copy in start(copies, sems):
        copy.wait()


def assemble(layout, out, parts):
    anywhere = pl.BlockSpec(memory_space=pl.ANY)
    shape = (layout.rows, layout.columns, layout.channels)
    args = ([] if out is None else [out]) + [part for part, *_ in parts]
    return pl.pallas_call(
        functools.partial(assemble_kernel, layout, [kind for _, *kind in parts]),
        out_shape=jax.ShapeDtypeStruct(shape, jnp.bfloat16),
        in_specs=([] if out is None else [anywhere]) + [VMEM] * len(parts),
        out_specs=anywhere,
        scratch_shapes=[pltpu.SemaphoreType.DMA((len(parts),))],
        input_output_aliases={} if out is None else {0: 0},
        compiler_params=PARAMS,
        cost_estimate=cost(1),
        name="assemble",
    )(*args)


def within(array):
    return lax.ppermute(array, "row", [(i, i ^ 1) for i in range(lax.axis_size("row"))])


def across(array):
    pairs = [(i, i + 1) for i in range(1, lax.axis_size("row") - 1, 2)]
    return lax.ppermute(array, "row", pairs + [(target, source) for source, target in pairs])


def swap_hid(array):
    return lax.ppermute(array, "hid", [(0, 1), (1, 0)])


def swap_row(array, bit):
    return lax.ppermute(array, "row", [(i, i ^ bit) for i in range(lax.axis_size("row"))])


def after(array, *earlier):
    return lax.optimization_barrier((array, *earlier))[0]


def gather(w_up, b_up, w_down):
    number, me = lax.axis_size("hid"), lax.axis_index("hid")
    arrays = [lax.all_gather(a, "hid") for a in (w_up, b_up.reshape(1, -1), w_down)]
    pick = lambda a, k: lax.dynamic_index_in_dim(a, lax.rem(me + k, number), 0, keepdims=False)
    return [pick(a, k) for k in range(1, number) for a in arrays]


def shards(features, dw_weight, dw_bias, ln_gain, ln_bias, w_up, b_up, w_down, b_down, layer_scale):
    layout = Layout(features, dw_weight)
    blocks, rows, number = layout.blocks, layout.rows, layout.number
    me, row, count = lax.axis_index("hid"), lax.axis_index("row"), lax.axis_size("row")
    odd = lax.rem(row, 2)
    pairs = number == 2 and w_up.shape[2] == 2 * layout.channels and count % 8 == 0
    weights = (w_up, b_up, w_down)
    norm, ending = (ln_gain, ln_bias), (b_down, layer_scale)

    outer, inner, *packed = prepare(layout, features, weights if pairs else ())
    far, near = across(outer), within(inner)
    state = features
    if pairs:
        up, down = swap_hid(packed[0]), swap_hid(packed[1])
    for b in range(blocks):
        before, *complete = conv_own(b, layout, state, near, dw_weight, dw_bias)
        if not pairs:
            kind, parts = "plain", gather(w_up[b], b_up[b], w_down[b])
        if b < blocks - 1:
            if pairs:
                later = swap_hid(pack(b + 1, layout, weights))
            if pairs and b == 0:
                down = after(down, before)
                up_other, down_other = swap_row(up, 4), swap_row(down, 4)
            chosen = layout.result_rows(b)
            x, total = conv_rest(b, layout, chosen, far, before, dw_weight, *norm, weights)
            if pairs and b == 0:
                up_other, down_other = after(up_other, total), after(down_other, total)
                mine = [up, down, up_other, down_other]
                kind, parts = "pairs", [within(a) for a in mine]
                biases = mine[::2], parts[::2]
                total = add(b, layout, x, total, kind, mine)
            elif pairs:
                kind, parts = "joined", [joined, *biases[0], within(joined), *biases[1]]
            state, outer, inner = more(
                b, layout, chosen, x, (total,), kind, parts, state, *ending, far
            )
            far, near = across(outer), within(inner)
            if pairs:
                joined = later
            continue
        first, last = tuple(range(before.shape[1])), tuple(range(before.shape[1], rows))
        x, total = conv_rest(b, layout, last, None, complete[0], dw_weight, *norm, weights)
        rest = None if pairs else parts
        if pairs and b == 0:
            kind, parts = "plain", gather(w_up[b], b_up[b], w_down[b])
            rest = parts
        elif pairs:
            joined = after(joined, total)
            kind, rest = "joined", [within(joined), *biases[1]]
            here = [joined, *biases[0]]
            parts = here + rest
            total = add(b, layout, x, total, kind, here)
        before = after(before, total)
        x_first, = conv_rest(b, layout, first, far, before, dw_weight, *norm)
        total = after(total, x_first)
        inner, = more(b, layout, last, x, (total,), kind, rest, state, *ending)
        outer, = more(b, layout, first, x_first, weights, kind, parts, state, *ending)
    if number == 2:
        later = swap_hid(inner), swap_hid(outer)
        out = assemble(layout, None, [(inner, 0, 0), (outer, 1, 0), (later[0], 0, 1)])
        return assemble(layout, out, [(later[1], 1, 1)])
    if number > 2:
        inner, outer = (lax.all_gather(a, "hid", axis=1, tiled=True) for a in (inner, outer))
    if inner.shape == outer.shape:
        return jnp.concatenate([jnp.where(odd == 1, inner, outer), jnp.where(odd == 1, outer, inner)])
    return jnp.where(odd == 1, jnp.concatenate([inner, outer]), jnp.concatenate([outer, inner]))


def solution(mesh):
    return jax.shard_map(
        shards,
        mesh=mesh,
        in_specs=(
            P("row", None, None),
            P(),
            P(),
            P(),
            P(),
            P(None, None, "hid"),
            P(None, "hid"),
            P(None, "hid", None),
            P(),
            P(),
        ),
        out_specs=P("row", None, None),
        check_vma=False,
    )
```
